256 devices in a mesh: pipe: 4 (over y), ctx: 8 (over z), tp: 8 (over x, core).
Axes of the slice: x: 4, y: 4, z: 8, core: 2. Of those that a mesh axis runs over, the one named last changes fastest.
Arguments:
- query_in: bfloat16 [4, 1024, 16384], P('pipe', 'ctx', 'tp'), may hold values from -200 to 200
- key_in: bfloat16 [4, 1024, 1024], P('pipe', ('ctx', 'tp')), may hold values from -7 to 7
- value_in: bfloat16 [4, 1024, 1024], P('pipe', ('ctx', 'tp')), may hold values from -6 to 6
- doc_ids: int32 [1024], replicated, may hold values from 0 to 7, never falling along the last dimension, each value on 1 to 512 neighbouring positions
- stretch_order: int32 [8], replicated, may hold values from 0 to 7, each once
- out_cot: bfloat16 [4, 1024, 16384], P('pipe', 'ctx', 'tp'), may hold values from -6 to 6
Outputs:
- attn_out: bfloat16 [4, 1024, 16384], P('pipe', 'ctx', 'tp')
- grad_query: bfloat16 [4, 1024, 16384], P('pipe', 'ctx', 'tp')
- grad_key: bfloat16 [4, 1024, 1024], P('pipe', ('ctx', 'tp'))
- grad_value: bfloat16 [4, 1024, 1024], P('pipe', ('ctx', 'tp'))
The draws below stay inside these ranges and needn't reach their ends.
Inputs may be any that keep to these rules, and one draw needn't show every extreme that they name: `doc_ids`: never falling along positions; each document spans 1 to 512 positions, one exactly 512. `stretch_order`: each block number appears once.
All inputs are finite; a program needn't handle non-finite values.
Results may differ from the reference program's by a relative error of at most 0.04.
Values may be sent and summed in bfloat16 or wider, within the bound.
No kernel may reach another device: no remote copies, remote signals or barrier semaphores. Data moves between devices by JAX's collectives and lax.ppermute only.
A program may use at most 128 MiB of HBM per device.

```python
import math
import jax
import jax.numpy as jnp
import numpy as np
from jax import lax

HEADS = 128
KV_HEADS = 8
HEAD_DIM = 128
TOK_DEV = 128
GROUP = 16
SEQ = 1024
LAYERS = 4
N_CTX = 8


def shared_keys(key):
    base_key = jax.random.fold_in(key, 0)
    shape = (LAYERS, SEQ, KV_HEADS, HEAD_DIM)
    base = jax.random.normal(base_key, shape, jnp.float32)
    mixed = base
    return jnp.clip(mixed, -6.5, 6.5)


def draw_key_in(key, part):
    keys = shared_keys(key)
    return keys.reshape(LAYERS, SEQ, KV_HEADS * HEAD_DIM).astype(jnp.bfloat16)


def draw_query_in(key, part):
    shape = (LAYERS, SEQ, KV_HEADS, GROUP, HEAD_DIM)
    own_key = jax.random.fold_in(key, 11)
    query = jnp.clip(1.5 * jax.random.normal(own_key, shape, jnp.float32), -9.0, 9.0)
    return query.reshape(LAYERS, SEQ, HEADS * HEAD_DIM).astype(jnp.bfloat16)


def shard_levels(key, shape, pieces, low, top_value):
    def one(dim, shards_of):
        steps = jax.random.uniform(jax.random.fold_in(jax.random.fold_in(key, 6), dim), (shards_of,), jnp.float32, low / len(pieces), top_value / len(pieces))
        return jnp.repeat(jnp.exp(steps), shape[dim] // shards_of).reshape((-1,) + (1,) * (len(shape) - dim - 1))

    factor_of = one(*pieces[0])
    for cut in pieces[1:]:
        factor_of = factor_of * one(*cut)
    return factor_of


def profile(count, total, reach, skew):
    weights = [(1 << 20) // math.isqrt(grade ** skew) + 1 for grade in range(2, count + 1)]
    spare, given = total - reach - (count - 1), [1] * (count - 1)
    while spare > 0:
        free = [i for i in range(count - 1) if given[i] < reach]
        whole, budget = sum([weights[i] for i in free]), spare
        for i in free:
            addition = min(reach - given[i], max(1, budget * weights[i] // whole), spare)
            given[i] = given[i] + addition
            spare = spare - addition
    return np.array([reach] + given)


def uneven(stream_key, number_of, total, reach, skew):
    if number_of == 2:
        one = jax.random.randint(stream_key, (), max(1, total - reach), min(reach, total - 1) + 1)
        return jnp.stack([one, total - one])
    lengths = jnp.asarray(profile(number_of, total, reach, skew), jnp.int32)
    twos = (number_of - 1) // 2
    donor, sink = lengths[1:1 + 2 * twos:2], lengths[2:2 + 2 * twos:2]
    slack = jnp.minimum(donor - 1, reach - sink)
    passed = jax.random.randint(jax.random.fold_in(stream_key, 1), (twos,), 0, 1 << 20) % (slack + 1)
    lengths = lengths.at[1:1 + 2 * twos:2].set(donor - passed).at[2:2 + 2 * twos:2].set(sink + passed)
    return lengths[jax.random.permutation(jax.random.fold_in(stream_key, 2), number_of)]


def scatter_about(key, extent, deviation, limit, cuts=(), kind=jnp.bfloat16):
    factor_of = shard_levels(key, extent, cuts, -0.22, 0.18) if cuts else 1.0
    values = jax.random.normal(key, extent, jnp.float32) * deviation * factor_of
    return jnp.minimum(jnp.maximum(values, -limit), limit).astype(kind)


def setup_inputs(seed: int = 0) -> dict:
    streams_of = jax.random.split(jax.random.key(seed), 7)
    query_in = draw_query_in(jax.random.fold_in(streams_of[6], 71), 0)
    key_in = draw_key_in(jax.random.fold_in(streams_of[6], 71), 0)
    value_in = scatter_about(streams_of[2], (LAYERS, SEQ, KV_HEADS * HEAD_DIM), 1.0, 6.0, ((0, 4), (1, 64)))
    doc_ids = jnp.searchsorted(jnp.cumsum(uneven(streams_of[3], N_CTX, SEQ, 4 * TOK_DEV, 1)), jnp.arange(SEQ), side="right").astype(jnp.int32)
    stretch_order = jax.random.permutation(streams_of[4], N_CTX).astype(jnp.int32)
    out_cot = scatter_about(streams_of[5], (LAYERS, SEQ, HEADS * HEAD_DIM), 1.0, 6.0, ((0, 4), (1, 8), (2, 8)))
    return {"query_in": query_in, "key_in": key_in, "value_in": value_in, "doc_ids": doc_ids, "stretch_order": stretch_order, "out_cot": out_cot}


masked_score = -1e30


def head_probs(query_g, key_g, allowed):
    scores = jnp.einsum("gqd,kd->gqk", query_g.astype(jnp.float32), key_g.astype(jnp.float32)) * (HEAD_DIM ** -0.5)
    scores = jnp.where(allowed[None], scores, masked_score)
    top = jnp.max(scores, axis=-1, keepdims=True)
    expo = jnp.exp(scores - top)
    return expo / jnp.sum(expo, axis=-1, keepdims=True)


def split_query(array):
    return array.reshape(SEQ, KV_HEADS, GROUP, HEAD_DIM).transpose(1, 2, 0, 3)


def merge_query(array):
    return array.transpose(2, 0, 1, 3).reshape(SEQ, HEADS * HEAD_DIM)


def split_keys(array):
    return array.reshape(SEQ, KV_HEADS, HEAD_DIM).transpose(1, 0, 2)


def merge_keys(array):
    return array.transpose(1, 0, 2).reshape(SEQ, KV_HEADS * HEAD_DIM)


def layer_forward(query, key_l, value_l, allowed):
    def one_head(operands):
        query_g, key_g, value_g = operands
        probs = head_probs(query_g, key_g, allowed)
        mixed = jnp.einsum("gqk,kd->gqd", probs.astype(jnp.bfloat16).astype(jnp.float32), value_g.astype(jnp.float32))
        return mixed.astype(jnp.bfloat16)

    return merge_query(lax.map(one_head, (split_query(query), split_keys(key_l), split_keys(value_l))))


def layer_backward(query, key_l, value_l, out_l, grad_out, allowed):
    scale = HEAD_DIM ** -0.5

    def one_head(operands):
        query_g, key_g, value_g, out_g, grad_g = operands
        probs = head_probs(query_g, key_g, allowed)
        grad_f = grad_g.astype(jnp.float32)
        grad_probs = jnp.einsum("gqd,kd->gqk", grad_f, value_g.astype(jnp.float32))
        delta = jnp.sum(grad_f * out_g.astype(jnp.float32), axis=-1, keepdims=True)
        grad_scores = (probs * (grad_probs - delta)).astype(jnp.bfloat16).astype(jnp.float32)
        grad_q = (jnp.einsum("gqk,kd->gqd", grad_scores, key_g.astype(jnp.float32)) * scale).astype(jnp.bfloat16)
        grad_k = jnp.einsum("gqk,gqd->kd", grad_scores, query_g.astype(jnp.float32)) * scale
        grad_v = jnp.einsum("gqk,gqd->kd", probs.astype(jnp.bfloat16).astype(jnp.float32), grad_f)
        return grad_q, grad_k.astype(jnp.bfloat16), grad_v.astype(jnp.bfloat16)

    grad_q, grad_k, grad_v = lax.map(one_head, (split_query(query), split_keys(key_l), split_keys(value_l), split_query(out_l), split_query(grad_out)))
    return merge_query(grad_q), merge_keys(grad_k), merge_keys(grad_v)


def reference(query_in, key_in, value_in, doc_ids, stretch_order, out_cot):
    rows = jnp.arange(SEQ, dtype=jnp.int32)
    starts = jnp.take(stretch_order, rows // TOK_DEV)
    position = (starts * TOK_DEV + rows % TOK_DEV).astype(jnp.int32)
    document = jnp.take(doc_ids, position)
    allowed = (position[None, :] <= position[:, None]) & (document[None, :] == document[:, None])
    incoming = jnp.zeros((SEQ, HEADS * HEAD_DIM), jnp.float32)
    queries = []
    outputs = []
    for layer in range(LAYERS):
        query = (query_in[layer].astype(jnp.float32) + incoming).astype(jnp.bfloat16)
        output = layer_forward(query, key_in[layer], value_in[layer], allowed)
        queries.append(query)
        outputs.append(output)
        incoming = output.astype(jnp.float32)
    grads_q = [None] * LAYERS
    grads_k = [None] * LAYERS
    grads_v = [None] * LAYERS
    returned = jnp.zeros((SEQ, HEADS * HEAD_DIM), jnp.float32)
    for layer in reversed(range(LAYERS)):
        grad_out = (out_cot[layer].astype(jnp.float32) + returned).astype(jnp.bfloat16)
        grad_q, grad_k, grad_v = layer_backward(queries[layer], key_in[layer], value_in[layer], outputs[layer], grad_out, allowed)
        grads_q[layer] = grad_q
        grads_k[layer] = grad_k
        grads_v[layer] = grad_v
        returned = grad_q.astype(jnp.float32)
    return jnp.stack(outputs), jnp.stack(grads_q), jnp.stack(grads_k), jnp.stack(grads_v)
```

```python
import functools
import math

import jax
import jax.numpy as jnp
from jax import lax
from jax.experimental import pallas as pl
from jax.experimental.pallas import tpu as pltpu
from jax.sharding import PartitionSpec as P

HEAD_DIM = 128
BLOCK = 128
REACH = 4
SPAN = (REACH + 1) * BLOCK
SCALE = HEAD_DIM ** (-0.5)
EXP2_SCALE = SCALE * math.log2(math.e)

masked_score = -1e30


def nt(a, b):
    return lax.dot_general(a, b, (((1,), (1,)), ((), ())), preferred_element_type=jnp.float32)


def nn(a, b):
    return lax.dot_general(a, b, (((1,), (0,)), ((), ())), preferred_element_type=jnp.float32)


def layers_kernel(
    place, query, cot, bias,
    k_own, k_next, k_far_a, k_far_b, k_prev, v_own, v_next, v_far_a, v_far_b, v_prev,
    out, grad_query, grad_kv,
    keys, values, expo, queries, scale_rows, gs_all, ds_all,
):
    layers, rows, width = query.shape
    heads = width // HEAD_DIM
    bf16, f32 = jnp.bfloat16, jnp.float32
    me = place[0]
    half = SPAN // 2
    for store, own, after, far_a, far_b, before in (
        (keys, k_own, k_next, k_far_a, k_far_b, k_prev),
        (values, v_own, v_next, v_far_a, v_far_b, v_prev),
    ):
        store[me] = own[...]
        store[(me + 1) % layers] = after[...]
        store[(me + 2) % layers, :half] = far_a[...]
        store[(me + 2) % layers, half:] = far_b[...]
        store[(me + 3) % layers] = before[...]

    def cols(h):
        return slice(h * HEAD_DIM, (h + 1) * HEAD_DIM)

    def span(h):
        return slice(h * rows, (h + 1) * rows)

    for l in range(layers):
        for h in range(heads):
            q = query[l, :, cols(h)]
            if l > 0:
                q = (q.astype(f32) + out[l - 1, :, cols(h)].astype(f32)).astype(bf16)
            queries[l, span(h)] = q
            t = nt(q, keys[l]) * EXP2_SCALE + bias[...]
            e = jnp.exp2(t - jnp.max(t, axis=-1, keepdims=True))
            r = 1.0 / jnp.sum(e, axis=-1, keepdims=True)
            e = e.astype(bf16)
            expo[l, span(h)] = e
            scale_rows[l, span(h)] = jnp.broadcast_to(r, (rows, HEAD_DIM))
            out[l, :, cols(h)] = (nn(e, values[l]) * r).astype(bf16)

    for l in reversed(range(layers)):
        for h in range(heads):
            g = cot[l, :, cols(h)]
            if l < layers - 1:
                g = (g.astype(f32) + grad_query[l + 1, :, cols(h)].astype(f32)).astype(bf16)
            gs = (g.astype(f32) * scale_rows[l, span(h)]).astype(bf16)
            gs_all[span(h)] = gs
            delta = jnp.sum(
                gs.astype(f32) * out[l, :, cols(h)].astype(f32), axis=-1, keepdims=True
            )
            ds = (expo[l, span(h)].astype(f32) * (nt(gs, values[l]) - delta)).astype(bf16)
            ds_all[span(h)] = ds
            grad_query[l, :, cols(h)] = (nn(ds, keys[l]) * SCALE).astype(bf16)
        gk = nn(queries[l].T, ds_all[...]) * SCALE
        gv = nn(gs_all[...].T, expo[l])
        grad_kv[l, :SPAN] = gk.T.astype(bf16)
        grad_kv[l, SPAN:] = gv.T.astype(bf16)


def run_layers(place, query, cot, bias, k_parts, v_parts):
    layers, rows, width = query.shape
    stacked = rows * width // HEAD_DIM
    bf16, f32 = jnp.bfloat16, jnp.float32
    vmem = pl.BlockSpec(memory_space=pltpu.VMEM)
    return pl.pallas_call(
        layers_kernel,
        out_shape=(
            jax.ShapeDtypeStruct((layers, rows, width), bf16),
            jax.ShapeDtypeStruct((layers, rows, width), bf16),
            jax.ShapeDtypeStruct((layers, 2 * SPAN, HEAD_DIM), bf16),
        ),
        in_specs=[pl.BlockSpec(memory_space=pltpu.SMEM)] + [vmem] * 13,
        out_specs=(vmem, vmem, vmem),
        scratch_shapes=[
            pltpu.VMEM((layers, SPAN, HEAD_DIM), bf16),
            pltpu.VMEM((layers, SPAN, HEAD_DIM), bf16),
            pltpu.VMEM((layers, stacked, SPAN), bf16),
            pltpu.VMEM((layers, stacked, HEAD_DIM), bf16),
            pltpu.VMEM((layers, stacked, HEAD_DIM), f32),
            pltpu.VMEM((stacked, HEAD_DIM), bf16),
            pltpu.VMEM((stacked, SPAN), bf16),
        ],
        compiler_params=pltpu.CompilerParams(vmem_limit_bytes=48 * 1024 * 1024),
        name="layers",
    )(place, query, cot, bias, *k_parts, *v_parts)


def moved(block, distance):
    size = lax.axis_size("pipe")
    return lax.ppermute(block, "pipe", [(i, (i + distance) % size) for i in range(size)])


def shards(query_in, key_in, value_in, doc_ids, stretch_order, out_cot):
    bf16, f32 = jnp.bfloat16, jnp.float32
    tp_count = lax.axis_size("tp")
    ctx_count = lax.axis_size("ctx")
    layers = lax.axis_size("pipe")
    layer = lax.axis_index("pipe")
    rows = query_in.shape[1]
    width = query_in.shape[2]
    part = width // layers
    kv_rows = key_in.shape[1]

    def spread(block):
        heads = block.reshape(kv_rows, tp_count, HEAD_DIM).transpose(1, 0, 2)
        sent = jnp.broadcast_to(heads[None], (ctx_count,) + heads.shape)
        sent = sent.reshape(ctx_count * tp_count, kv_rows, HEAD_DIM)
        got = lax.all_to_all(sent, ("ctx", "tp"), split_axis=0, concat_axis=0, tiled=True)
        return got.reshape(ctx_count, BLOCK, HEAD_DIM)

    keys_all = spread(key_in[0])
    values_all = spread(value_in[0])

    position = stretch_order[lax.axis_index("ctx")]
    block_ids = jnp.arange(ctx_count, dtype=jnp.int32)
    holder = jnp.sum(
        jnp.where(stretch_order[None, :] == block_ids[:, None], block_ids[None, :], 0), axis=1
    )

    def window(blocks):
        return jnp.concatenate(
            [
                lax.dynamic_index_in_dim(
                    blocks, holder[jnp.maximum(position - REACH + j, 0)], 0, keepdims=False
                )
                for j in range(REACH + 1)
            ]
        )

    def gathered(own):
        half = SPAN // 2
        before = moved(own, 1)
        after = moved(own, -1)
        far_a = moved(before[:half], 1)
        far_b = moved(after[half:], -1)
        return (own, after, far_a, far_b, before)

    k_parts = gathered(window(keys_all))
    v_parts = gathered(window(values_all))

    offsets = jnp.arange(SPAN, dtype=jnp.int32)
    row_ids = jnp.arange(rows, dtype=jnp.int32)
    documents = jnp.concatenate([jnp.full((REACH * BLOCK,), -1, jnp.int32), doc_ids])
    near_documents = lax.dynamic_slice_in_dim(documents, position * BLOCK, SPAN)
    own_documents = near_documents[REACH * BLOCK:]
    allowed = (offsets[None, :] <= row_ids[:, None] + REACH * BLOCK) & (
        near_documents[None, :] == own_documents[:, None]
    )
    bias = jnp.where(allowed, 0.0, masked_score).astype(f32)

    def to_layers(block):
        return lax.all_to_all(
            block.reshape(rows, layers, part).transpose(1, 0, 2), "pipe", 0, 0, tiled=True
        )

    def to_owner(blocks):
        got = lax.all_to_all(blocks, "pipe", 0, 0, tiled=True)
        return got.transpose(1, 0, 2).reshape(1, rows, width)

    query = to_layers(query_in[0])
    cot = to_layers(out_cot[0])
    out, grad_query, grad_kv = run_layers(
        layer.reshape(1), query, cot, bias, k_parts, v_parts
    )

    def part_of(distance):
        return lax.dynamic_index_in_dim(grad_kv, (layer + distance) % layers, 0, keepdims=False)

    own, after, far, before = (part_of(d) for d in range(4))
    half = SPAN
    from_before = moved(far[:half], 1)
    from_after = moved(far[half:], -1)

    def add(a, b):
        return (a.astype(f32) + b.astype(f32)).astype(bf16)

    up = jnp.concatenate([add(after[:half], from_before), after[half:]])
    down = jnp.concatenate([before[:half], add(before[half:], from_after)])
    total = own.astype(f32) + moved(up, 1).astype(f32) + moved(down, -1).astype(f32)
    total = total.astype(bf16).reshape(2, REACH + 1, BLOCK, HEAD_DIM)

    def placed(b):
        j = stretch_order[b] - (position - REACH)
        block = lax.dynamic_index_in_dim(total, jnp.clip(j, 0, REACH), 1, keepdims=False)
        return jnp.where((j >= 0) & (j <= REACH), block, jnp.zeros_like(block))

    sent = jnp.stack([placed(b) for b in range(ctx_count)])
    sent = sent.reshape(ctx_count, 2, tp_count, kv_rows, HEAD_DIM).transpose(0, 2, 1, 3, 4)
    sent = sent.reshape(ctx_count * tp_count, 2 * kv_rows, HEAD_DIM)
    got = lax.all_to_all(sent, ("ctx", "tp"), split_axis=0, concat_axis=0, tiled=True)
    got = got.reshape(ctx_count, tp_count, 2, kv_rows, HEAD_DIM)
    grads = jnp.sum(got.astype(f32), axis=0).astype(bf16)
    grads = grads.transpose(1, 2, 0, 3).reshape(2, 1, kv_rows, tp_count * HEAD_DIM)
    return (to_owner(out), to_owner(grad_query), grads[0], grads[1])


def solution(mesh):
    return jax.shard_map(
        shards,
        mesh=mesh,
        in_specs=(
            P("pipe", "ctx", "tp"),
            P("pipe", ("ctx", "tp"), None),
            P("pipe", ("ctx", "tp"), None),
            P(),
            P(),
            P("pipe", "ctx", "tp"),
        ),
        out_specs=(
            P("pipe", "ctx", "tp"),
            P("pipe", "ctx", "tp"),
            P("pipe", ("ctx", "tp"), None),
            P("pipe", ("ctx", "tp"), None),
        ),
        check_vma=False,
    )
```

```python
import math

import jax
import jax.numpy as jnp
from jax import lax
from jax.experimental import pallas as pl
from jax.experimental.pallas import tpu as pltpu
from jax.sharding import PartitionSpec as P

HEAD_DIM = 128
BLOCK = 128
REACH = 4
NEAR = REACH + 1
SPAN = NEAR * BLOCK
LAYERS = 4
TILE = 16
SUBS = BLOCK // TILE
SCALE = HEAD_DIM ** (-0.5)
EXP2_SCALE = SCALE * math.log2(math.e)

masked_score = -1e30
bf16 = jnp.bfloat16
f32 = jnp.float32
ANY = pl.BlockSpec(memory_space=pl.ANY)
VMEM = pl.BlockSpec(memory_space=pltpu.VMEM)
SMEM = pl.BlockSpec(memory_space=pltpu.SMEM)
PARAMS = pltpu.CompilerParams(vmem_limit_bytes=48 * 1024 * 1024)


def shape(*dims, dtype=bf16):
    return jax.ShapeDtypeStruct(dims, dtype)


def nt(a, b):
    return lax.dot_general(a, b, (((1,), (1,)), ((), ())), preferred_element_type=f32)


def nn(a, b):
    return lax.dot_general(a, b, (((1,), (0,)), ((), ())), preferred_element_type=f32)


def spread_kernel(key, value, sent):
    ctx_count = sent.shape[0] // SUBS
    for t in range(SUBS):
        cols = slice(t * HEAD_DIM, (t + 1) * HEAD_DIM)
        k, v = key[:, cols], value[:, cols]
        for c in range(ctx_count):
            sent[c * SUBS + t, :TILE] = k
            sent[c * SUBS + t, TILE:] = v


def spread(key, value, ctx_count):
    return pl.pallas_call(
        spread_kernel,
        out_shape=shape(ctx_count * SUBS, 2 * TILE, HEAD_DIM),
        in_specs=[VMEM, VMEM],
        out_specs=VMEM,
        compiler_params=PARAMS,
        name="spread",
    )(key, value)


def layers_kernel(
    bias_in, kv_own, kv_next, kv_far_a, kv_far_b, kv_prev, qc_own, qc_next, qc_far, qc_prev,
    dkv_own, dkv_next, dkv_far_a, dkv_far_b, dkv_prev, og_own, og_next, og_far, og_prev,
    bias, kv, qc, og, dkv, keys, values, expo, queries, scale_rows, gs_all, ds_all, sems, out_sems,
):
    layers, _, rows, width = qc.shape
    heads = width // HEAD_DIM
    me = lax.axis_index("pipe")
    half = kv.shape[1] // 2

    def slot(d):
        return lax.rem(me + d, layers)

    pairs = [
        (kv_own, kv.at[slot(0)]),
        (kv_next, kv.at[slot(1)]),
        (kv_far_a, kv.at[slot(2), pl.ds(0, half)]),
        (kv_far_b, kv.at[slot(2), pl.ds(half, half)]),
        (kv_prev, kv.at[slot(3)]),
        (qc_own, qc.at[slot(0)]),
        (qc_next, qc.at[slot(1)]),
        (qc_far, qc.at[slot(2)]),
        (qc_prev, qc.at[slot(3)]),
        (bias_in, bias),
    ]
    copies = [pltpu.make_async_copy(a, b, sems.at[i]) for i, (a, b) in enumerate(pairs)]
    for copy in copies:
        copy.start()
    for copy in copies:
        copy.wait()
    for l in range(layers):
        keys[l] = kv[l, :, :TILE].reshape(SPAN, HEAD_DIM)
        values[l] = kv[l, :, TILE:].reshape(SPAN, HEAD_DIM)

    def cols(h):
        return slice(h * HEAD_DIM, (h + 1) * HEAD_DIM)

    def span(h):
        return slice(h * rows, (h + 1) * rows)

    for l in range(layers):
        for h in range(heads):
            q = qc[l, 0, :, cols(h)]
            if l > 0:
                q = (q.astype(f32) + og[l - 1, 0, :, cols(h)].astype(f32)).astype(bf16)
            queries[l, span(h)] = q
            t = nt(q, keys[l]) * EXP2_SCALE + bias[...]
            e = jnp.exp2(t - jnp.max(t, axis=-1, keepdims=True))
            r = 1.0 / jnp.sum(e, axis=-1, keepdims=True)
            e = e.astype(bf16)
            expo[l, span(h)] = e
            scale_rows[l, span(h)] = jnp.broadcast_to(r, (rows, HEAD_DIM))
            og[l, 0, :, cols(h)] = (nn(e, values[l]) * r).astype(bf16)

    for l in reversed(range(layers)):
        for h in range(heads):
            g = qc[l, 1, :, cols(h)]
            if l < layers - 1:
                g = (g.astype(f32) + og[l + 1, 1, :, cols(h)].astype(f32)).astype(bf16)
            gs = (g.astype(f32) * scale_rows[l, span(h)]).astype(bf16)
            gs_all[span(h)] = gs
            delta = jnp.sum(
                gs.astype(f32) * og[l, 0, :, cols(h)].astype(f32), axis=-1, keepdims=True
            )
            ds = (expo[l, span(h)].astype(f32) * (nt(gs, values[l]) - delta)).astype(bf16)
            ds_all[span(h)] = ds
            og[l, 1, :, cols(h)] = (nn(ds, keys[l]) * SCALE).astype(bf16)
        gk = nn(queries[l].T, ds_all[...]) * SCALE
        gv = nn(gs_all[...].T, expo[l])
        dkv[l, :, :TILE] = gk.T.astype(bf16).reshape(SPAN // TILE, TILE, HEAD_DIM)
        dkv[l, :, TILE:] = gv.T.astype(bf16).reshape(SPAN // TILE, TILE, HEAD_DIM)

    pairs = [
        (dkv.at[slot(2), pl.ds(0, half)], dkv_far_a),
        (dkv.at[slot(2), pl.ds(half, half)], dkv_far_b),
        (dkv.at[slot(1)], dkv_next),
        (dkv.at[slot(3)], dkv_prev),
        (dkv.at[slot(0)], dkv_own),
        (og.at[slot(0)], og_own),
        (og.at[slot(1)], og_next),
        (og.at[slot(2)], og_far),
        (og.at[slot(3)], og_prev),
    ]
    copies = [pltpu.make_async_copy(a, b, out_sems.at[i]) for i, (a, b) in enumerate(pairs)]
    for copy in copies:
        copy.start()
    for copy in copies:
        copy.wait()


def run_layers(bias, kv_parts, qc_parts):
    _, rows, width = qc_parts[0].shape
    stacked = rows * width // HEAD_DIM
    tiles = SPAN // TILE
    kv_shape = shape(tiles, 2 * TILE, HEAD_DIM)
    kv_half = shape(tiles // 2, 2 * TILE, HEAD_DIM)
    qc_shape = shape(2, rows, width)
    return pl.pallas_call(
        layers_kernel,
        out_shape=(kv_shape, kv_shape, kv_half, kv_half, kv_shape) + (qc_shape,) * LAYERS,
        in_specs=[ANY] * 10,
        out_specs=(ANY,) * 9,
        scratch_shapes=[
            pltpu.VMEM((rows, SPAN), f32),
            pltpu.VMEM((LAYERS, tiles, 2 * TILE, HEAD_DIM), bf16),
            pltpu.VMEM((LAYERS, 2, rows, width), bf16),
            pltpu.VMEM((LAYERS, 2, rows, width), bf16),
            pltpu.VMEM((LAYERS, tiles, 2 * TILE, HEAD_DIM), bf16),
            pltpu.VMEM((LAYERS, SPAN, HEAD_DIM), bf16),
            pltpu.VMEM((LAYERS, SPAN, HEAD_DIM), bf16),
            pltpu.VMEM((LAYERS, stacked, SPAN), bf16),
            pltpu.VMEM((LAYERS, stacked, HEAD_DIM), bf16),
            pltpu.VMEM((LAYERS, stacked, HEAD_DIM), f32),
            pltpu.VMEM((stacked, HEAD_DIM), bf16),
            pltpu.VMEM((stacked, SPAN), bf16),
            pltpu.SemaphoreType.DMA((10,)),
            pltpu.SemaphoreType.DMA((9,)),
        ],
        compiler_params=PARAMS,
        name="layers",
    )(bias, *kv_parts, *qc_parts)


def place_kernel(order, own_in, up_in, down_in, sent, own, up, down, sems):
    pairs = [(own_in, own), (up_in, up), (down_in, down)]
    copies = [pltpu.make_async_copy(a, b, sems.at[i]) for i, (a, b) in enumerate(pairs)]
    for copy in copies:
        copy.start()
    for copy in copies:
        copy.wait()
    first = order[lax.axis_index("ctx")] - REACH
    for c in range(sent.shape[0] // SUBS):
        j = order[c] - first
        near = (j >= 0) & (j <= REACH)
        at = pl.ds(pl.multiple_of(jnp.clip(j, 0, REACH) * SUBS, SUBS), SUBS)

        @pl.when(near)
        def _():
            total = own[at].astype(f32) + up[at].astype(f32) + down[at].astype(f32)
            sent[c * SUBS:(c + 1) * SUBS] = total.astype(bf16)

        @pl.when(jnp.logical_not(near))
        def _():
            sent[c * SUBS:(c + 1) * SUBS] = jnp.zeros((SUBS, 2 * TILE, HEAD_DIM), bf16)


def place(order, own, up, down):
    return pl.pallas_call(
        place_kernel,
        out_shape=shape(order.shape[0] * SUBS, 2 * TILE, HEAD_DIM),
        in_specs=[SMEM, ANY, ANY, ANY],
        out_specs=VMEM,
        scratch_shapes=[pltpu.VMEM(own.shape, bf16)] * 3 + [pltpu.SemaphoreType.DMA((3,))],
        compiler_params=PARAMS,
        name="place",
    )(order, own, up, down)


def total_kernel(got_in, grad_key, grad_value, got, sem):
    copy = pltpu.make_async_copy(got_in, got, sem)
    copy.start()
    copy.wait()
    for t in range(SUBS):
        total = got[t].astype(f32)
        for c in range(1, got.shape[0] // SUBS):
            total = total + got[c * SUBS + t].astype(f32)
        total = total.astype(bf16)
        cols = slice(t * HEAD_DIM, (t + 1) * HEAD_DIM)
        grad_key[:, cols] = total[:TILE]
        grad_value[:, cols] = total[TILE:]


def total(got):
    return pl.pallas_call(
        total_kernel,
        out_shape=(shape(TILE, SUBS * HEAD_DIM),) * 2,
        in_specs=[ANY],
        out_specs=(VMEM, VMEM),
        scratch_shapes=[pltpu.VMEM(got.shape, bf16), pltpu.SemaphoreType.DMA],
        compiler_params=PARAMS,
        name="total",
    )(got)


def assemble_kernel(own, prev, far, after, out, grad_query, sems):
    me = lax.axis_index("pipe")
    width = own.shape[2]
    copies = []
    for d, piece in enumerate((own, prev, far, after)):
        column = pl.multiple_of(lax.rem(me + LAYERS - d, LAYERS) * width, width)
        for i, whole in enumerate((out, grad_query)):
            copies.append(
                pltpu.make_async_copy(
                    piece.at[i], whole.at[:, pl.ds(column, width)], sems.at[2 * d + i]
                )
            )
    for copy in copies:
        copy.start()
    for copy in copies:
        copy.wait()


def assemble(pieces):
    _, rows, width = pieces[0].shape
    return pl.pallas_call(
        assemble_kernel,
        out_shape=(shape(rows, LAYERS * width),) * 2,
        in_specs=[ANY] * 4,
        out_specs=(ANY, ANY),
        scratch_shapes=[pltpu.SemaphoreType.DMA((8,))],
        compiler_params=PARAMS,
        name="assemble",
    )(*pieces)


def moved(block, distance):
    size = lax.axis_size("pipe")
    return lax.ppermute(block, "pipe", [(i, (i + distance) % size) for i in range(size)])


def exchanged(block, axes):
    return lax.all_to_all(block, axes, split_axis=0, concat_axis=0, tiled=True)


def shards(query_in, key_in, value_in, doc_ids, stretch_order, out_cot):
    ctx_count = lax.axis_size("ctx")
    layer = lax.axis_index("pipe")
    rows = query_in.shape[1]
    part = query_in.shape[2] // LAYERS

    got = exchanged(spread(key_in[0], value_in[0], ctx_count), ("ctx", "tp"))

    def piece(distance):
        start = lax.rem(layer + distance, LAYERS) * part
        return jnp.stack(
            [
                lax.dynamic_slice(
                    x[0], (0, start), (rows, part), allow_negative_indices=False
                )
                for x in (query_in, out_cot)
            ]
        )

    qc_parts = [piece(0), moved(piece(3), 3), moved(piece(2), 2), moved(piece(1), 1)]

    position = stretch_order[lax.axis_index("ctx")]
    block_ids = jnp.arange(ctx_count, dtype=jnp.int32)
    wanted = jnp.maximum(position - REACH + jnp.arange(NEAR, dtype=jnp.int32), 0)
    holder = jnp.sum(
        jnp.where(stretch_order[None, :] == wanted[:, None], block_ids[None, :], 0), axis=1
    )
    own = jnp.concatenate(
        [
            lax.dynamic_slice(
                got, (holder[j] * SUBS, 0, 0), (SUBS, 2 * TILE, HEAD_DIM),
                allow_negative_indices=False,
            )
            for j in range(NEAR)
        ]
    )
    half = own.shape[0] // 2
    before = moved(own, 1)
    after = moved(own, -1)
    far_a = moved(before[:half], 1)
    far_b = moved(after[half:], -1)

    offsets = jnp.arange(SPAN, dtype=jnp.int32)
    row_ids = jnp.arange(rows, dtype=jnp.int32)
    documents = jnp.concatenate([jnp.full((REACH * BLOCK,), -1, jnp.int32), doc_ids])
    near_documents = lax.dynamic_slice(
        documents, (position * BLOCK,), (SPAN,), allow_negative_indices=False
    )
    own_documents = near_documents[REACH * BLOCK:]
    allowed = (offsets[None, :] <= row_ids[:, None] + REACH * BLOCK) & (
        near_documents[None, :] == own_documents[:, None]
    )
    bias = jnp.where(allowed, 0.0, masked_score).astype(f32)

    (
        dkv_own, dkv_next, dkv_far_a, dkv_far_b, dkv_prev, og_own, og_next, og_far, og_prev
    ) = run_layers(bias, (own, after, far_a, far_b, before), qc_parts)

    from_before = moved(dkv_far_a, 1)
    from_after = moved(dkv_far_b, -1)

    def add(a, b):
        return (a.astype(f32) + b.astype(f32)).astype(bf16)

    up = jnp.concatenate([add(dkv_next[:half], from_before), dkv_next[half:]])
    down = jnp.concatenate([dkv_prev[:half], add(dkv_prev[half:], from_after)])
    sent = place(stretch_order, dkv_own, moved(up, 1), moved(down, -1))
    grad_key, grad_value = total(exchanged(sent, ("ctx", "tp")))
    out, grad_query = assemble([og_own, moved(og_next, 1), moved(og_far, 2), moved(og_prev, 3)])
    return (out[None], grad_query[None], grad_key[None], grad_value[None])


def solution(mesh):
    return jax.shard_map(
        shards,
        mesh=mesh,
        in_specs=(
            P("pipe", "ctx", "tp"),
            P("pipe", ("ctx", "tp"), None),
            P("pipe", ("ctx", "tp"), None),
            P(),
            P(),
            P("pipe", "ctx", "tp"),
        ),
        out_specs=(
            P("pipe", "ctx", "tp"),
            P("pipe", "ctx", "tp"),
            P("pipe", ("ctx", "tp"), None),
            P("pipe", ("ctx", "tp"), None),
        ),
        check_vma=False,
    )
```

```python
import math

import jax
import jax.numpy as jnp
from jax import lax
from jax.experimental import pallas as pl
from jax.experimental.pallas import tpu as pltpu
from jax.sharding import PartitionSpec as P

HEAD_DIM = 128
BLOCK = 128
REACH = 4
NEAR = REACH + 1
SPAN = NEAR * BLOCK
LAYERS = 4
TILE = 16
SUBS = BLOCK // TILE
SCALE = HEAD_DIM ** (-0.5)
EXP2_SCALE = SCALE * math.log2(math.e)

masked_score = -1e30
bf16 = jnp.bfloat16
f32 = jnp.float32
ANY = pl.BlockSpec(memory_space=pl.ANY)
VMEM = pl.BlockSpec(memory_space=pltpu.VMEM)
SMEM = pl.BlockSpec(memory_space=pltpu.SMEM)
PARAMS = pltpu.CompilerParams(vmem_limit_bytes=48 * 1024 * 1024)


def shape(*dims, dtype=bf16):
    return jax.ShapeDtypeStruct(dims, dtype)


def nt(a, b):
    return lax.dot_general(a, b, (((1,), (1,)), ((), ())), preferred_element_type=f32)


def nn(a, b):
    return lax.dot_general(a, b, (((1,), (0,)), ((), ())), preferred_element_type=f32)


def spread_kernel(key_in, value_in, sent, key, value, sems):
    ctx_count = sent.shape[0] // SUBS
    copies = [
        pltpu.make_async_copy(key_in, key, sems.at[0]),
        pltpu.make_async_copy(value_in, value, sems.at[1]),
    ]
    for copy in copies:
        copy.start()
    for copy in copies:
        copy.wait()
    for t in range(SUBS):
        rows = key if t % 2 == 0 else value
        for j in range(2):
            head = t // 2 * 2 + j
            block = rows[:, head * HEAD_DIM:(head + 1) * HEAD_DIM]
            for c in range(ctx_count):
                sent[c * SUBS + t, j * TILE:(j + 1) * TILE] = block


def spread(key, value, ctx_count):
    return pl.pallas_call(
        spread_kernel,
        out_shape=shape(ctx_count * SUBS, 2 * TILE, HEAD_DIM),
        in_specs=[ANY, ANY],
        out_specs=VMEM,
        scratch_shapes=[pltpu.VMEM(key.shape, bf16)] * 2 + [pltpu.SemaphoreType.DMA((2,))],
        compiler_params=PARAMS,
        name="spread",
    )(key, value)


def run_copies(pairs, sems):
    copies = [pltpu.make_async_copy(a, b, sems.at[i]) for i, (a, b) in enumerate(pairs)]
    for copy in copies:
        copy.start()
    for copy in copies:
        copy.wait()


def place_of():
    pipe = lax.axis_index("pipe")
    core = lax.rem(lax.axis_index("tp"), 2)
    return pipe, core, lax.rem(pipe, 2) * 2 + core


def layers_kernel(
    bias_in, a0, a1, a2, a3, b0, b1, b2, b3, q0, q1, q2, q3,
    keep, give, og0, og1, og2, og3,
    bias, kv, qc, og, dkv, expo, queries, scale_rows, gs_all, ds_all, sems, out_sems,
):
    layers, _, rows, width = qc.shape
    heads = width // HEAD_DIM
    pipe, core, group = place_of()

    def back(start, d):
        return lax.rem(start + layers - d, layers)

    run_copies(
        [(x, kv.at[core, back(pipe, d)]) for d, x in enumerate((a0, a1, a2, a3))]
        + [(x, kv.at[1 - core, back(pipe, d)]) for d, x in enumerate((b0, b1, b2, b3))]
        + [(x, qc.at[back(group, m)]) for m, x in enumerate((q0, q1, q2, q3))]
        + [(bias_in, bias)],
        sems,
    )

    def cols(h):
        return slice(h * HEAD_DIM, (h + 1) * HEAD_DIM)

    def span(h):
        return slice(h * rows, (h + 1) * rows)

    for l in range(layers):
        for h in range(heads):
            q = qc[l, 0, :, cols(h)]
            if l > 0:
                q = (q.astype(f32) + og[l - 1, 0, :, cols(h)].astype(f32)).astype(bf16)
            queries[l, span(h)] = q
            t = nt(q, kv[0, l]) * EXP2_SCALE + bias[...]
            e = jnp.exp2(t - jnp.max(t, axis=-1, keepdims=True))
            r = 1.0 / jnp.sum(e, axis=-1, keepdims=True)
            e = e.astype(bf16)
            expo[l, span(h)] = e
            scale_rows[l, span(h)] = jnp.broadcast_to(r, (rows, HEAD_DIM))
            og[l, 0, :, cols(h)] = (nn(e, kv[1, l]) * r).astype(bf16)

    for l in reversed(range(layers)):
        for h in range(heads):
            g = qc[l, 1, :, cols(h)]
            if l < layers - 1:
                g = (g.astype(f32) + og[l + 1, 1, :, cols(h)].astype(f32)).astype(bf16)
            gs = (g.astype(f32) * scale_rows[l, span(h)]).astype(bf16)
            gs_all[span(h)] = gs
            delta = jnp.sum(
                gs.astype(f32) * og[l, 0, :, cols(h)].astype(f32), axis=-1, keepdims=True
            )
            ds = (expo[l, span(h)].astype(f32) * (nt(gs, kv[1, l]) - delta)).astype(bf16)
            ds_all[span(h)] = ds
            og[l, 1, :, cols(h)] = (nn(ds, kv[0, l]) * SCALE).astype(bf16)
        gk = nn(queries[l].T, ds_all[...]) * SCALE
        gv = nn(gs_all[...].T, expo[l])
        dkv[0, l] = gk.T.astype(bf16)
        dkv[1, l] = gv.T.astype(bf16)

    run_copies(
        [(dkv.at[1 - core, lax.rem(pipe + d, layers)], give.at[d]) for d in range(layers)]
        + [(dkv.at[core, lax.rem(pipe + d, layers)], keep.at[d]) for d in range(layers)]
        + [(og.at[back(group, m)], x) for m, x in enumerate((og0, og1, og2, og3))],
        out_sems,
    )


def run_layers(bias, mine, theirs, qc_parts):
    _, rows, width = qc_parts[0].shape
    stacked = rows * width // HEAD_DIM
    kv_shape = shape(LAYERS, SPAN, HEAD_DIM)
    return pl.pallas_call(
        layers_kernel,
        out_shape=(kv_shape, kv_shape) + (shape(2, rows, width),) * LAYERS,
        in_specs=[ANY] * 13,
        out_specs=(ANY,) * 6,
        scratch_shapes=[
            pltpu.VMEM((rows, SPAN), f32),
            pltpu.VMEM((2, LAYERS, SPAN, HEAD_DIM), bf16),
            pltpu.VMEM((LAYERS, 2, rows, width), bf16),
            pltpu.VMEM((LAYERS, 2, rows, width), bf16),
            pltpu.VMEM((2, LAYERS, SPAN, HEAD_DIM), bf16),
            pltpu.VMEM((LAYERS, stacked, SPAN), bf16),
            pltpu.VMEM((LAYERS, stacked, HEAD_DIM), bf16),
            pltpu.VMEM((LAYERS, stacked, HEAD_DIM), f32),
            pltpu.VMEM((stacked, HEAD_DIM), bf16),
            pltpu.VMEM((stacked, SPAN), bf16),
            pltpu.SemaphoreType.DMA((13,)),
            pltpu.SemaphoreType.DMA((12,)),
        ],
        compiler_params=PARAMS,
        name="layers",
    )(bias, *mine, *theirs, *qc_parts)


def place_kernel(order, p0, p1, p2, p3, sent, parts, sems):
    pipe, _, _ = place_of()
    run_copies(
        [
            (x, parts.at[lax.rem(pipe + LAYERS - d, LAYERS)])
            for d, x in enumerate((p0, p1, p2, p3))
        ],
        sems,
    )
    first = order[lax.axis_index("ctx")] - REACH
    for c in range(sent.shape[0] // SUBS):
        j = order[c] - first
        near = (j >= 0) & (j <= REACH)
        at = pl.ds(pl.multiple_of(jnp.clip(j, 0, REACH) * BLOCK, BLOCK), BLOCK)

        @pl.when(near)
        def _():
            for head in range(2):
                total = parts[2 * head, at].astype(f32) + parts[2 * head + 1, at].astype(f32)
                sent[c * SUBS:(c + 1) * SUBS, head * TILE:(head + 1) * TILE] = total.astype(
                    bf16
                ).reshape(SUBS, TILE, HEAD_DIM)

        @pl.when(jnp.logical_not(near))
        def _():
            sent[c * SUBS:(c + 1) * SUBS] = jnp.zeros((SUBS, 2 * TILE, HEAD_DIM), bf16)


def place(order, parts):
    return pl.pallas_call(
        place_kernel,
        out_shape=shape(order.shape[0] * SUBS, 2 * TILE, HEAD_DIM),
        in_specs=[SMEM] + [ANY] * LAYERS,
        out_specs=VMEM,
        scratch_shapes=[
            pltpu.VMEM((LAYERS, SPAN, HEAD_DIM), bf16), pltpu.SemaphoreType.DMA((LAYERS,))
        ],
        compiler_params=PARAMS,
        name="place",
    )(order, *parts)


def total_kernel(got_in, grad_key, grad_value, got, sem):
    copy = pltpu.make_async_copy(got_in, got, sem)
    copy.start()
    copy.wait()
    for t in range(SUBS):
        total = got[t].astype(f32)
        for c in range(1, got.shape[0] // SUBS):
            total = total + got[c * SUBS + t].astype(f32)
        total = total.astype(bf16)
        whole = grad_key if t % 2 == 0 else grad_value
        for j in range(2):
            head = t // 2 * 2 + j
            whole[:, head * HEAD_DIM:(head + 1) * HEAD_DIM] = total[j * TILE:(j + 1) * TILE]


def total(got):
    return pl.pallas_call(
        total_kernel,
        out_shape=(shape(TILE, SUBS * HEAD_DIM),) * 2,
        in_specs=[ANY],
        out_specs=(VMEM, VMEM),
        scratch_shapes=[pltpu.VMEM(got.shape, bf16), pltpu.SemaphoreType.DMA],
        compiler_params=PARAMS,
        name="total",
    )(got)


def assemble_kernel(g0, g1, g2, g3, out, grad_query, sems):
    me = lax.axis_index("pipe")
    width = g0.shape[2]
    pairs = []
    for m, piece in enumerate((g0, g1, g2, g3)):
        column = pl.multiple_of(lax.rem(me + m, LAYERS) * width, width)
        for i, whole in enumerate((out, grad_query)):
            pairs.append((piece.at[i], whole.at[:, pl.ds(column, width)]))
    run_copies(pairs, sems)


def assemble(pieces):
    _, rows, width = pieces[0].shape
    return pl.pallas_call(
        assemble_kernel,
        out_shape=(shape(rows, LAYERS * width),) * 2,
        in_specs=[ANY] * 4,
        out_specs=(ANY, ANY),
        scratch_shapes=[pltpu.SemaphoreType.DMA((8,))],
        compiler_params=PARAMS,
        name="assemble",
    )(*pieces)


def moved(block, distance):
    size = lax.axis_size("pipe")
    return lax.ppermute(block, "pipe", [(i, (i + distance) % size) for i in range(size)])


def swapped(block):
    size = lax.axis_size("tp")
    return lax.ppermute(block, "tp", [(i, i ^ 1) for i in range(size)])


def group_pairs(m):
    tp_count = lax.axis_size("tp")
    pairs = []
    for l in range(LAYERS):
        for tp in range(tp_count):
            group = (l + m) % LAYERS
            pipe = 2 * (tp % 2) + group // 2
            pairs.append((l * tp_count + tp, pipe * tp_count + tp - tp % 2 + group % 2))
    return pairs


def exchanged(block, axes):
    return lax.all_to_all(block, axes, split_axis=0, concat_axis=0, tiled=True)


def cut(block, starts, sizes):
    return lax.dynamic_slice(block, starts, sizes, allow_negative_indices=False)


def shards(query_in, key_in, value_in, doc_ids, stretch_order, out_cot):
    ctx_count = lax.axis_size("ctx")
    layer = lax.axis_index("pipe")
    rows = query_in.shape[1]
    part = query_in.shape[2] // LAYERS

    got = exchanged(spread(key_in[0], value_in[0], ctx_count), ("ctx", "tp"))

    qc_parts = []
    for m in range(LAYERS):
        start = lax.rem(layer + m, LAYERS) * part
        piece = jnp.stack([cut(x[0], (0, start), (rows, part)) for x in (query_in, out_cot)])
        qc_parts.append(lax.ppermute(piece, ("pipe", "tp"), group_pairs(m)))

    position = stretch_order[lax.axis_index("ctx")]
    block_ids = jnp.arange(ctx_count, dtype=jnp.int32)
    wanted = jnp.maximum(position - REACH + jnp.arange(NEAR, dtype=jnp.int32), 0)
    holder = jnp.sum(
        jnp.where(stretch_order[None, :] == wanted[:, None], block_ids[None, :], 0), axis=1
    )

    def window(distance):
        head = lax.rem(layer + distance, LAYERS) // 2
        return jnp.concatenate(
            [
                cut(got, (holder[j] * SUBS, head * TILE, 0), (SUBS, TILE, HEAD_DIM))
                for j in range(NEAR)
            ]
        ).reshape(SPAN, HEAD_DIM)

    mine = [window(0)] + [moved(window(d), d) for d in (1, 3, 2)]
    mine = [mine[0], mine[1], mine[3], mine[2]]
    theirs = [swapped(x) for x in mine]

    offsets = jnp.arange(SPAN, dtype=jnp.int32)
    row_ids = jnp.arange(rows, dtype=jnp.int32)
    documents = jnp.concatenate([jnp.full((REACH * BLOCK,), -1, jnp.int32), doc_ids])
    near_documents = cut(documents, (position * BLOCK,), (SPAN,))
    own_documents = near_documents[REACH * BLOCK:]
    allowed = (offsets[None, :] <= row_ids[:, None] + REACH * BLOCK) & (
        near_documents[None, :] == own_documents[:, None]
    )
    bias = jnp.where(allowed, 0.0, masked_score).astype(f32)

    keep, give, *groups = run_layers(bias, mine, theirs, qc_parts)
    received = swapped(give)
    sums = [
        (keep[d].astype(f32) + received[d].astype(f32)).astype(bf16) for d in range(LAYERS)
    ]
    parts = [sums[0]] + [moved(sums[d], d) for d in (1, 3, 2)]
    parts = [parts[0], parts[1], parts[3], parts[2]]
    grad_key, grad_value = total(exchanged(place(stretch_order, parts), ("ctx", "tp")))
    pieces = [
        lax.ppermute(x, ("pipe", "tp"), [(b, a) for a, b in group_pairs(m)])
        for m, x in enumerate(groups)
    ]
    out, grad_query = assemble(pieces)
    return (out[None], grad_query[None], grad_key[None], grad_value[None])


def solution(mesh):
    return jax.shard_map(
        shards,
        mesh=mesh,
        in_specs=(
            P("pipe", "ctx", "tp"),
            P("pipe", ("ctx", "tp"), None),
            P("pipe", ("ctx", "tp"), None),
            P(),
            P(),
            P("pipe", "ctx", "tp"),
        ),
        out_specs=(
            P("pipe", "ctx", "tp"),
            P("pipe", "ctx", "tp"),
            P("pipe", ("ctx", "tp"), None),
            P("pipe", ("ctx", "tp"), None),
        ),
        check_vma=False,
    )
```

```python
import math

import jax
import jax.numpy as jnp
from jax import lax
from jax.experimental import pallas as pl
from jax.experimental.pallas import tpu as pltpu
from jax.sharding import PartitionSpec as P

HEAD_DIM = 128
BLOCK = 128
REACH = 4
NEAR = REACH + 1
SPAN = NEAR * BLOCK
LAYERS = 4
TILE = 16
CORES = 2
TILES = BLOCK // TILE // CORES
SCALE = HEAD_DIM ** (-0.5)
EXP2_SCALE = SCALE * math.log2(math.e)

masked_score = -1e30
bf16 = jnp.bfloat16
f32 = jnp.float32
ANY = pl.BlockSpec(memory_space=pl.ANY)
HBM = pl.BlockSpec(memory_space=pltpu.HBM)
VMEM = pl.BlockSpec(memory_space=pltpu.VMEM)
SMEM = pl.BlockSpec(memory_space=pltpu.SMEM)
PARAMS = pltpu.CompilerParams(vmem_limit_bytes=48 * 1024 * 1024)


def shape(*dims, dtype=bf16):
    return jax.ShapeDtypeStruct(dims, dtype)


def nt(a, b):
    return lax.dot_general(a, b, (((1,), (1,)), ((), ())), preferred_element_type=f32)


def nn(a, b):
    return lax.dot_general(a, b, (((1,), (0,)), ((), ())), preferred_element_type=f32)


def run_copies(pairs, sems, meanwhile=None):
    copies = [pltpu.make_async_copy(a, b, sems.at[i]) for i, (a, b) in enumerate(pairs)]
    for copy in copies:
        copy.start()
    if meanwhile is not None:
        meanwhile()
    for copy in copies:
        copy.wait()


def place_of():
    pipe = lax.axis_index("pipe")
    core = lax.rem(lax.axis_index("tp"), CORES)
    return pipe, core, lax.rem(pipe, 2) * CORES + core


def spread_kernel(key_in, value_in, sent, key, value, sems):
    ctx_count = sent.shape[0] // TILES
    run_copies([(key_in, key), (value_in, value)], sems)
    for x in range(TILES):
        for kind, rows in enumerate((key, value)):
            for j in range(2):
                head = 2 * x + j
                block = rows[:, head * HEAD_DIM:(head + 1) * HEAD_DIM]
                for c in range(ctx_count):
                    sent[c * TILES + x, kind, j] = block


def spread(key, value, ctx_count):
    return pl.pallas_call(
        spread_kernel,
        out_shape=shape(ctx_count * TILES, 2, 2, TILE, HEAD_DIM),
        in_specs=[HBM, HBM],
        out_specs=VMEM,
        scratch_shapes=[pltpu.VMEM(key.shape, bf16)] * 2 + [pltpu.SemaphoreType.DMA((2,))],
        compiler_params=PARAMS,
        name="spread",
    )(key, value)


def pieces_kernel(query, cot, p0, p1, p2, p3, sems):
    me = lax.axis_index("pipe")
    width = p0.shape[2]
    pairs = []
    for m, piece in enumerate((p0, p1, p2, p3)):
        column = pl.multiple_of(lax.rem(me + m, LAYERS) * width, width)
        for i, whole in enumerate((query, cot)):
            pairs.append((whole.at[:, pl.ds(column, width)], piece.at[i]))
    run_copies(pairs, sems)


def pieces_of(query, cot):
    rows, width = query.shape
    return pl.pallas_call(
        pieces_kernel,
        out_shape=(shape(2, rows, width // LAYERS),) * LAYERS,
        in_specs=[HBM, HBM],
        out_specs=(ANY,) * LAYERS,
        scratch_shapes=[pltpu.SemaphoreType.DMA((2 * LAYERS,))],
        compiler_params=PARAMS,
        name="pieces",
    )(query, cot)


def layers_kernel(
    bias_in, a0, a1, a2, a3, b0, b1, b2, b3, q0, q1, q2, q3,
    keep, give, og0, og1, og2, og3,
    bias, kv, qc, og, dkv, expo, queries, scale_rows, gs_all, ds_all, sems, out_sems,
):
    layers, _, rows, width = qc.shape
    heads = width // HEAD_DIM
    pipe, core, group = place_of()

    def back(start, d):
        return lax.rem(start + layers - d, layers)

    pairs = []
    for k in range(2):
        for d, x in enumerate((a0, a1, a2, a3)):
            pairs.append((x.at[:, k], kv.at[k, back(pipe, d), :, core]))
        for d, x in enumerate((b0, b1, b2, b3)):
            pairs.append((x.at[:, k], kv.at[k, back(pipe, d), :, 1 - core]))
    for m, x in enumerate((q0, q1, q2, q3)):
        pairs.append((x, qc.at[back(group, m)]))
    pairs.append((bias_in, bias))
    run_copies(pairs, sems)

    def cols(h):
        return slice(h * HEAD_DIM, (h + 1) * HEAD_DIM)

    def span(h):
        return slice(h * rows, (h + 1) * rows)

    def keys(l):
        return kv[0, l].reshape(SPAN, HEAD_DIM)

    def values(l):
        return kv[1, l].reshape(SPAN, HEAD_DIM)

    ones = jnp.ones((SPAN, HEAD_DIM), bf16)
    for l in range(layers):
        for h in range(heads):
            q = qc[l, 0, :, cols(h)]
            if l > 0:
                q = (q.astype(f32) + og[l - 1, 0, :, cols(h)].astype(f32)).astype(bf16)
            queries[l, span(h)] = q
            t = nt(q, keys(l)) * EXP2_SCALE + bias[...]
            e = jnp.exp2(t - jnp.max(t, axis=-1, keepdims=True)).astype(bf16)
            expo[l, span(h)] = e
            mixed = nn(e, jnp.concatenate([values(l), ones], axis=1))
            r = 1.0 / mixed[:, HEAD_DIM:]
            scale_rows[l, span(h)] = r
            og[l, 0, :, cols(h)] = (mixed[:, :HEAD_DIM] * r).astype(bf16)

    def probs_grad(l, h):
        g = qc[l, 1, :, cols(h)]
        if l < layers - 1:
            g = (g.astype(f32) + og[l + 1, 1, :, cols(h)].astype(f32)).astype(bf16)
        gs = (g.astype(f32) * scale_rows[l, span(h)]).astype(bf16)
        gs_all[l, span(h)] = gs
        delta = jnp.sum(gs.astype(f32) * og[l, 0, :, cols(h)].astype(f32), axis=-1, keepdims=True)
        return nt(gs, values(l)), delta

    def scores_grad(l, h, dp, delta):
        ds = (expo[l, span(h)].astype(f32) * (dp - delta)).astype(bf16)
        ds_all[l, span(h)] = ds
        return ds

    def query_grad(l, h, ds):
        og[l, 1, :, cols(h)] = (nn(ds, keys(l)) * SCALE).astype(bf16)
        if h == heads - 1:
            gk = nn(queries[l].T, ds_all[l]) * SCALE
            gv = nn(gs_all[l].T, expo[l])
            dkv[0, l] = gk.T.astype(bf16).reshape(NEAR * TILES, CORES, TILE, HEAD_DIM)
            dkv[1, l] = gv.T.astype(bf16).reshape(NEAR * TILES, CORES, TILE, HEAD_DIM)

    steps = [(l, h) for l in reversed(range(layers)) for h in range(heads)]
    first, second = {}, {}
    for i in range(len(steps) + 2):
        if i < len(steps):
            first[i] = probs_grad(*steps[i])
        if 1 <= i <= len(steps):
            second[i - 1] = scores_grad(*steps[i - 1], *first.pop(i - 1))
        if i >= 2:
            query_grad(*steps[i - 2], second.pop(i - 2))

    pairs = []
    for d in range(layers):
        l = lax.rem(pipe + d, layers)
        for k in range(2):
            pairs.append((dkv.at[k, l, :, 1 - core], give.at[d, k]))
            pairs.append((dkv.at[k, l, :, core], keep.at[d, k]))
    for m, x in enumerate((og0, og1, og2, og3)):
        pairs.append((og.at[back(group, m)], x))
    run_copies(pairs, out_sems)


def run_layers(bias, mine, theirs, qc_parts):
    _, rows, width = qc_parts[0].shape
    stacked = rows * width // HEAD_DIM
    kv_shape = shape(LAYERS, 2, NEAR * TILES, TILE, HEAD_DIM)
    return pl.pallas_call(
        layers_kernel,
        out_shape=(kv_shape, kv_shape) + (shape(2, rows, width),) * LAYERS,
        in_specs=[ANY] * 13,
        out_specs=(ANY,) * 6,
        scratch_shapes=[
            pltpu.VMEM((rows, SPAN), f32),
            pltpu.VMEM((2, LAYERS, NEAR * TILES, CORES, TILE, HEAD_DIM), bf16),
            pltpu.VMEM((LAYERS, 2, rows, width), bf16),
            pltpu.VMEM((LAYERS, 2, rows, width), bf16),
            pltpu.VMEM((2, LAYERS, NEAR * TILES, CORES, TILE, HEAD_DIM), bf16),
            pltpu.VMEM((LAYERS, stacked, SPAN), bf16),
            pltpu.VMEM((LAYERS, stacked, HEAD_DIM), bf16),
            pltpu.VMEM((LAYERS, stacked, HEAD_DIM), f32),
            pltpu.VMEM((LAYERS, stacked, HEAD_DIM), bf16),
            pltpu.VMEM((LAYERS, stacked, SPAN), bf16),
            pltpu.SemaphoreType.DMA((21,)),
            pltpu.SemaphoreType.DMA((20,)),
        ],
        compiler_params=PARAMS,
        name="layers",
    )(bias, *mine, *theirs, *qc_parts)


def place_kernel(order, p0, p1, p2, p3, sent, parts, sems):
    pipe, _, _ = place_of()

    def clear():
        sent[...] = jnp.zeros(sent.shape, bf16)

    run_copies(
        [
            (x, parts.at[lax.rem(pipe + LAYERS - d, LAYERS)])
            for d, x in enumerate((p0, p1, p2, p3))
        ],
        sems,
        clear,
    )
    first = order[lax.axis_index("ctx")] - REACH
    for c in range(sent.shape[0] // TILES):
        j = order[c] - first

        @pl.when((j >= 0) & (j <= REACH))
        def _():
            at = pl.ds(j * TILES, TILES)
            for head in range(2):
                total = parts[2 * head, :, at].astype(f32) + parts[2 * head + 1, :, at].astype(f32)
                total = total.astype(bf16)
                for k in range(2):
                    sent[c * TILES:(c + 1) * TILES, k, head] = total[k]


def place(order, parts):
    return pl.pallas_call(
        place_kernel,
        out_shape=shape(order.shape[0] * TILES, 2, 2, TILE, HEAD_DIM),
        in_specs=[SMEM] + [ANY] * LAYERS,
        out_specs=VMEM,
        scratch_shapes=[
            pltpu.VMEM((LAYERS,) + parts[0].shape, bf16), pltpu.SemaphoreType.DMA((LAYERS,))
        ],
        compiler_params=PARAMS,
        name="place",
    )(order, *parts)


def total_kernel(got_in, grad_key, grad_value, got, sem):
    copy = pltpu.make_async_copy(got_in, got, sem)
    copy.start()
    copy.wait()
    for x in range(TILES):
        total = got[x].astype(f32)
        for c in range(1, got.shape[0] // TILES):
            total = total + got[c * TILES + x].astype(f32)
        total = total.astype(bf16)
        for kind, whole in enumerate((grad_key, grad_value)):
            for j in range(2):
                head = 2 * x + j
                whole[:, head * HEAD_DIM:(head + 1) * HEAD_DIM] = total[kind, j]


def total(got):
    return pl.pallas_call(
        total_kernel,
        out_shape=(shape(TILE, TILES * 2 * HEAD_DIM),) * 2,
        in_specs=[ANY],
        out_specs=(VMEM, VMEM),
        scratch_shapes=[pltpu.VMEM(got.shape, bf16), pltpu.SemaphoreType.DMA],
        compiler_params=PARAMS,
        name="total",
    )(got)


def assemble_kernel(g0, g1, g2, g3, out, grad_query, sems):
    me = lax.axis_index("pipe")
    width = g0.shape[2]
    pairs = []
    for m, piece in enumerate((g0, g1, g2, g3)):
        column = pl.multiple_of(lax.rem(me + m, LAYERS) * width, width)
        for i, whole in enumerate((out, grad_query)):
            pairs.append((piece.at[i], whole.at[:, pl.ds(column, width)]))
    run_copies(pairs, sems)


def assemble(pieces):
    _, rows, width = pieces[0].shape
    return pl.pallas_call(
        assemble_kernel,
        out_shape=(shape(rows, LAYERS * width),) * 2,
        in_specs=[ANY] * 4,
        out_specs=(ANY, ANY),
        scratch_shapes=[pltpu.SemaphoreType.DMA((8,))],
        compiler_params=PARAMS,
        name="assemble",
    )(*pieces)


def moved(block, distance):
    size = lax.axis_size("pipe")
    return lax.ppermute(block, "pipe", [(i, (i + distance) % size) for i in range(size)])


def swapped(block):
    size = lax.axis_size("tp")
    return lax.ppermute(block, "tp", [(i, i ^ 1) for i in range(size)])


def group_pairs(m):
    tp_count = lax.axis_size("tp")
    pairs = []
    for l in range(LAYERS):
        for tp in range(tp_count):
            group = (l + m) % LAYERS
            pipe = 2 * (tp % 2) + group // 2
            pairs.append((l * tp_count + tp, pipe * tp_count + tp - tp % 2 + group % 2))
    return pairs


def exchanged(block):
    ctx_count, tp_count = lax.axis_size("ctx"), lax.axis_size("tp")
    groups = [
        [c * tp_count + tp for c in range(ctx_count) for tp in range(core, tp_count, CORES)]
        for core in range(CORES)
    ]
    flat = block.reshape(block.shape[0], -1, HEAD_DIM)
    got = lax.all_to_all(
        flat, ("ctx", "tp"), split_axis=0, concat_axis=0, axis_index_groups=groups, tiled=True
    )
    return got.reshape(block.shape)


def cut(block, starts, sizes):
    return lax.dynamic_slice(block, starts, sizes, allow_negative_indices=False)


def shards(query_in, key_in, value_in, doc_ids, stretch_order, out_cot):
    ctx_count = lax.axis_size("ctx")
    layer = lax.axis_index("pipe")
    rows = query_in.shape[1]

    got = exchanged(spread(key_in[0], value_in[0], ctx_count))
    qc_parts = [
        lax.ppermute(piece, ("pipe", "tp"), group_pairs(m))
        for m, piece in enumerate(pieces_of(query_in[0], out_cot[0]))
    ]

    position = stretch_order[lax.axis_index("ctx")]
    block_ids = jnp.arange(ctx_count, dtype=jnp.int32)
    wanted = jnp.maximum(position - REACH + jnp.arange(NEAR, dtype=jnp.int32), 0)
    holder = jnp.sum(
        jnp.where(stretch_order[None, :] == wanted[:, None], block_ids[None, :], 0), axis=1
    )

    def window(distance):
        head = lax.rem(layer + distance, LAYERS) // 2
        return jnp.concatenate(
            [
                cut(got, (holder[j] * TILES, 0, head, 0, 0), (TILES, 2, 1, TILE, HEAD_DIM))
                for j in range(NEAR)
            ]
        ).reshape(NEAR * TILES, 2, TILE, HEAD_DIM)

    mine = [window(0)] + [moved(window(d), d) for d in (1, 3, 2)]
    mine = [mine[0], mine[1], mine[3], mine[2]]
    theirs = [swapped(x) for x in mine]

    offsets = jnp.arange(SPAN, dtype=jnp.int32)
    row_ids = jnp.arange(rows, dtype=jnp.int32)
    documents = jnp.concatenate([jnp.full((REACH * BLOCK,), -1, jnp.int32), doc_ids])
    near_documents = cut(documents, (position * BLOCK,), (SPAN,))
    own_documents = near_documents[REACH * BLOCK:]
    allowed = (offsets[None, :] <= row_ids[:, None] + REACH * BLOCK) & (
        near_documents[None, :] == own_documents[:, None]
    )
    bias = jnp.where(allowed, 0.0, masked_score).astype(f32)

    keep, give, *groups = run_layers(bias, mine, theirs, qc_parts)
    received = swapped(give)
    sums = [
        (keep[d].astype(f32) + received[d].astype(f32)).astype(bf16) for d in range(LAYERS)
    ]
    parts = [sums[0]] + [moved(sums[d], d) for d in (1, 3, 2)]
    parts = [parts[0], parts[1], parts[3], parts[2]]
    grad_key, grad_value = total(exchanged(place(stretch_order, parts)))
    out, grad_query = assemble(
        [
            lax.ppermute(x, ("pipe", "tp"), [(b, a) for a, b in group_pairs(m)])
            for m, x in enumerate(groups)
        ]
    )
    return (out[None], grad_query[None], grad_key[None], grad_value[None])


def solution(mesh):
    return jax.shard_map(
        shards,
        mesh=mesh,
        in_specs=(
            P("pipe", "ctx", "tp"),
            P("pipe", ("ctx", "tp"), None),
            P("pipe", ("ctx", "tp"), None),
            P(),
            P(),
            P("pipe", "ctx", "tp"),
        ),
        out_specs=(
            P("pipe", "ctx", "tp"),
            P("pipe", "ctx", "tp"),
            P("pipe", ("ctx", "tp"), None),
            P("pipe", ("ctx", "tp"), None),
        ),
        check_vma=False,
    )
```

```python
import math

import jax
import jax.numpy as jnp
from jax import lax
from jax.experimental import pallas as pl
from jax.experimental.pallas import tpu as pltpu
from jax.sharding import PartitionSpec as P

HEAD_DIM = 128
BLOCK = 128
REACH = 4
NEAR = REACH + 1
SPAN = NEAR * BLOCK
LAYERS = 4
TILE = 16
CORES = 2
TILES = BLOCK // TILE // CORES
SCALE = HEAD_DIM ** (-0.5)
EXP2_SCALE = SCALE * math.log2(math.e)

masked_score = -1e30
bf16 = jnp.bfloat16
f32 = jnp.float32
ANY = pl.BlockSpec(memory_space=pl.ANY)
HBM = pl.BlockSpec(memory_space=pltpu.HBM)
VMEM = pl.BlockSpec(memory_space=pltpu.VMEM)
SMEM = pl.BlockSpec(memory_space=pltpu.SMEM)
PARAMS = pltpu.CompilerParams(vmem_limit_bytes=48 * 1024 * 1024)


def shape(*dims, dtype=bf16):
    return jax.ShapeDtypeStruct(dims, dtype)


def nt(a, b):
    return lax.dot_general(a, b, (((1,), (1,)), ((), ())), preferred_element_type=f32)


def nn(a, b):
    return lax.dot_general(a, b, (((1,), (0,)), ((), ())), preferred_element_type=f32)


def run_copies(pairs, sems, meanwhile=None):
    copies = [pltpu.make_async_copy(a, b, sems.at[i]) for i, (a, b) in enumerate(pairs)]
    for copy in copies:
        copy.start()
    if meanwhile is not None:
        meanwhile()
    for copy in copies:
        copy.wait()


def place_of():
    pipe = lax.axis_index("pipe")
    core = lax.rem(lax.axis_index("tp"), CORES)
    return pipe, core, lax.rem(pipe, 2) * CORES + core


def spread_kernel(kv_in, sent, kv, tiles, sem, sems):
    count = tiles.shape[0]
    run_copies([(kv_in, kv)], sem)
    for x in range(count):
        for kind in range(2):
            for j in range(2):
                head = 2 * x + j
                tiles[x, kind, j] = kv[kind, :, head * HEAD_DIM:(head + 1) * HEAD_DIM]
    run_copies(
        [(tiles, sent.at[pl.ds(c * count, count)]) for c in range(sent.shape[0] // count)], sems
    )


def spread(kv, ctx_count):
    return pl.pallas_call(
        spread_kernel,
        out_shape=shape(ctx_count * TILES, 2, 2, TILE, HEAD_DIM),
        in_specs=[ANY],
        out_specs=ANY,
        scratch_shapes=[
            pltpu.VMEM(kv.shape, bf16),
            pltpu.VMEM((TILES, 2, 2, TILE, HEAD_DIM), bf16),
            pltpu.SemaphoreType.DMA((1,)),
            pltpu.SemaphoreType.DMA((ctx_count,)),
        ],
        compiler_params=PARAMS,
        name="spread",
    )(kv)


LAYER_OF = ((1, 2, 0, 3), (3, 0, 1, 2), (2, 1, 3, 0), (0, 3, 2, 1))
GROUP_OF = tuple(tuple(row.index(l) for l in range(LAYERS)) for row in LAYER_OF)


def chosen(row, index):
    value = jnp.int32(row[0])
    for i in range(1, len(row)):
        value = jnp.where(index == i, row[i], value)
    return value


def group_of(m):
    pipe, core, _ = place_of()
    return chosen(GROUP_OF[m], lax.rem(pipe + 2 * core, LAYERS))


def layer_of(m):
    pipe, _, group = place_of()
    return lax.rem(chosen(LAYER_OF[m], group) + 2 * (pipe // 2), LAYERS)


def pieces_kernel(query, cot, p0, p1, p2, p3, sems):
    width = p0.shape[2]
    pairs = []
    for m, piece in enumerate((p0, p1, p2, p3)):
        column = pl.multiple_of(group_of(m) * width, width)
        for i, whole in enumerate((query, cot)):
            pairs.append((whole.at[:, pl.ds(column, width)], piece.at[i]))
    run_copies(pairs, sems)


def pieces_of(query, cot):
    rows, width = query.shape
    return pl.pallas_call(
        pieces_kernel,
        out_shape=(shape(2, rows, width // LAYERS),) * LAYERS,
        in_specs=[HBM, HBM],
        out_specs=(ANY,) * LAYERS,
        scratch_shapes=[pltpu.SemaphoreType.DMA((2 * LAYERS,))],
        compiler_params=PARAMS,
        name="pieces",
    )(query, cot)


def layers_kernel(
    bias_in, a0, a1, a2, a3, b0, b1, b2, b3, q0, q1, q2, q3,
    keep, give, og0, og1, og2, og3,
    bias, kv, qc, og, dkv, expo, queries, scale_rows, gs_all, ds_all, sems, out_sems,
):
    layers, _, rows, width = qc.shape
    heads = width // HEAD_DIM
    pipe, core, group = place_of()

    def back(start, d):
        return lax.rem(start + layers - d, layers)

    pairs = []
    for k in range(2):
        for d, x in enumerate((a0, a1, a2, a3)):
            pairs.append((x.at[:, k], kv.at[k, back(pipe, d), :, core]))
        for d, x in enumerate((b0, b1, b2, b3)):
            pairs.append((x.at[:, k], kv.at[k, back(pipe, d), :, 1 - core]))
    for m, x in enumerate((q0, q1, q2, q3)):
        pairs.append((x, qc.at[layer_of(m)]))
    pairs.append((bias_in, bias))
    run_copies(pairs, sems)

    def cols(h):
        return slice(h * HEAD_DIM, (h + 1) * HEAD_DIM)

    def span(h):
        return slice(h * rows, (h + 1) * rows)

    def keys(l):
        return kv[0, l].reshape(SPAN, HEAD_DIM)

    def values(l):
        return kv[1, l].reshape(SPAN, HEAD_DIM)

    ones = jnp.ones((SPAN, HEAD_DIM), bf16)
    for l in range(layers):
        for h in range(heads):
            q = qc[l, 0, :, cols(h)]
            if l > 0:
                q = (q.astype(f32) + og[l - 1, 0, :, cols(h)].astype(f32)).astype(bf16)
            queries[l, span(h)] = q
            t = nt(q, keys(l)) * EXP2_SCALE + bias[...]
            e = jnp.exp2(t - jnp.max(t, axis=-1, keepdims=True)).astype(bf16)
            expo[l, span(h)] = e
            mixed = nn(e, jnp.concatenate([values(l), ones], axis=1))
            r = 1.0 / mixed[:, HEAD_DIM:]
            scale_rows[l, span(h)] = r
            og[l, 0, :, cols(h)] = (mixed[:, :HEAD_DIM] * r).astype(bf16)

    def probs_grad(l, h):
        g = qc[l, 1, :, cols(h)]
        if l < layers - 1:
            g = (g.astype(f32) + og[l + 1, 1, :, cols(h)].astype(f32)).astype(bf16)
        gs = (g.astype(f32) * scale_rows[l, span(h)]).astype(bf16)
        gs_all[l, span(h)] = gs
        delta = jnp.sum(gs.astype(f32) * og[l, 0, :, cols(h)].astype(f32), axis=-1, keepdims=True)
        return nt(gs, values(l)), delta

    def scores_grad(l, h, dp, delta):
        ds = (expo[l, span(h)].astype(f32) * (dp - delta)).astype(bf16)
        ds_all[l, span(h)] = ds
        return ds

    def query_grad(l, h, ds):
        og[l, 1, :, cols(h)] = (nn(ds, keys(l)) * SCALE).astype(bf16)
        if h == heads - 1:
            gk = nn(queries[l].T, ds_all[l]) * SCALE
            gv = nn(gs_all[l].T, expo[l])
            dkv[0, l] = gk.T.astype(bf16).reshape(NEAR * TILES, CORES, TILE, HEAD_DIM)
            dkv[1, l] = gv.T.astype(bf16).reshape(NEAR * TILES, CORES, TILE, HEAD_DIM)

    steps = [(l, h) for l in reversed(range(layers)) for h in range(heads)]
    first, second = {}, {}
    for i in range(len(steps) + 2):
        if i < len(steps):
            first[i] = probs_grad(*steps[i])
        if 1 <= i <= len(steps):
            second[i - 1] = scores_grad(*steps[i - 1], *first.pop(i - 1))
        if i >= 2:
            query_grad(*steps[i - 2], second.pop(i - 2))

    pairs = []
    for d in range(layers):
        l = lax.rem(pipe + d, layers)
        for k in range(2):
            pairs.append((dkv.at[k, l, :, 1 - core], give.at[d, k]))
            pairs.append((dkv.at[k, l, :, core], keep.at[d, k]))
    for m, x in enumerate((og0, og1, og2, og3)):
        pairs.append((og.at[layer_of(m)], x))
    run_copies(pairs, out_sems)


def run_layers(bias, mine, theirs, qc_parts):
    _, rows, width = qc_parts[0].shape
    stacked = rows * width // HEAD_DIM
    kv_shape = shape(LAYERS, 2, NEAR * TILES, TILE, HEAD_DIM)
    return pl.pallas_call(
        layers_kernel,
        out_shape=(kv_shape, kv_shape) + (shape(2, rows, width),) * LAYERS,
        in_specs=[ANY] * 13,
        out_specs=(ANY,) * 6,
        scratch_shapes=[
            pltpu.VMEM((rows, SPAN), f32),
            pltpu.VMEM((2, LAYERS, NEAR * TILES, CORES, TILE, HEAD_DIM), bf16),
            pltpu.VMEM((LAYERS, 2, rows, width), bf16),
            pltpu.VMEM((LAYERS, 2, rows, width), bf16),
            pltpu.VMEM((2, LAYERS, NEAR * TILES, CORES, TILE, HEAD_DIM), bf16),
            pltpu.VMEM((LAYERS, stacked, SPAN), bf16),
            pltpu.VMEM((LAYERS, stacked, HEAD_DIM), bf16),
            pltpu.VMEM((LAYERS, stacked, HEAD_DIM), f32),
            pltpu.VMEM((LAYERS, stacked, HEAD_DIM), bf16),
            pltpu.VMEM((LAYERS, stacked, SPAN), bf16),
            pltpu.SemaphoreType.DMA((21,)),
            pltpu.SemaphoreType.DMA((20,)),
        ],
        compiler_params=PARAMS,
        name="layers",
    )(bias, *mine, *theirs, *qc_parts)


def place_kernel(order_in, p0, p1, p2, p3, sent_out, order, parts, sent, sems, out_sems):
    pipe, _, _ = place_of()

    def clear():
        sent[...] = jnp.zeros(sent.shape, bf16)

    run_copies(
        [(order_in, order)]
        + [
            (x, parts.at[lax.rem(pipe + LAYERS - d, LAYERS)])
            for d, x in enumerate((p0, p1, p2, p3))
        ],
        sems,
        clear,
    )
    first = order[lax.axis_index("ctx")] - REACH
    for c in range(sent.shape[0] // TILES):
        j = order[c] - first

        @pl.when((j >= 0) & (j <= REACH))
        def _():
            at = pl.ds(j * TILES, TILES)
            for head in range(2):
                total = parts[2 * head, :, at].astype(f32) + parts[2 * head + 1, :, at].astype(f32)
                total = total.astype(bf16)
                for k in range(2):
                    sent[c * TILES:(c + 1) * TILES, k, head] = total[k]

    run_copies([(sent, sent_out)], out_sems)


def place(order, parts):
    return pl.pallas_call(
        place_kernel,
        out_shape=shape(order.shape[0] * TILES, 2, 2, TILE, HEAD_DIM),
        in_specs=[ANY] * (1 + LAYERS),
        out_specs=ANY,
        scratch_shapes=[
            pltpu.SMEM(order.shape, jnp.int32),
            pltpu.VMEM((LAYERS,) + parts[0].shape, bf16),
            pltpu.VMEM((order.shape[0] * TILES, 2, 2, TILE, HEAD_DIM), bf16),
            pltpu.SemaphoreType.DMA((1 + LAYERS,)),
            pltpu.SemaphoreType.DMA((1,)),
        ],
        compiler_params=PARAMS,
        name="place",
    )(order, *parts)


def total_kernel(got_in, grad_key, grad_value, got, sem):
    copy = pltpu.make_async_copy(got_in, got, sem)
    copy.start()
    copy.wait()
    for x in range(TILES):
        total = got[x].astype(f32)
        for c in range(1, got.shape[0] // TILES):
            total = total + got[c * TILES + x].astype(f32)
        total = total.astype(bf16)
        for kind, whole in enumerate((grad_key, grad_value)):
            for j in range(2):
                head = 2 * x + j
                whole[:, head * HEAD_DIM:(head + 1) * HEAD_DIM] = total[kind, j]


def total(got):
    return pl.pallas_call(
        total_kernel,
        out_shape=(shape(TILE, TILES * 2 * HEAD_DIM),) * 2,
        in_specs=[ANY],
        out_specs=(VMEM, VMEM),
        scratch_shapes=[pltpu.VMEM(got.shape, bf16), pltpu.SemaphoreType.DMA],
        compiler_params=PARAMS,
        name="total",
    )(got)


def assemble_kernel(g0, g1, g2, g3, out, grad_query, sems):
    width = g0.shape[2]
    pairs = []
    for m, piece in enumerate((g0, g1, g2, g3)):
        column = pl.multiple_of(group_of(m) * width, width)
        for i, whole in enumerate((out, grad_query)):
            pairs.append((piece.at[i], whole.at[:, pl.ds(column, width)]))
    run_copies(pairs, sems)


def assemble(pieces):
    _, rows, width = pieces[0].shape
    return pl.pallas_call(
        assemble_kernel,
        out_shape=(shape(rows, LAYERS * width),) * 2,
        in_specs=[ANY] * 4,
        out_specs=(ANY, ANY),
        scratch_shapes=[pltpu.SemaphoreType.DMA((8,))],
        compiler_params=PARAMS,
        name="assemble",
    )(*pieces)


def moved(block, distance):
    size = lax.axis_size("pipe")
    return lax.ppermute(block, "pipe", [(i, (i + distance) % size) for i in range(size)])


def swapped(block):
    size = lax.axis_size("tp")
    return lax.ppermute(block, "tp", [(i, i ^ 1) for i in range(size)])


def sent_over(block, pairs):
    tp_count = lax.axis_size("tp")
    route = [
        (a * tp_count + x + b, c * tp_count + x + d)
        for (a, b), (c, d) in pairs
        for x in range(0, tp_count, CORES)
    ]
    return lax.ppermute(block, ("pipe", "tp"), route)


def round_pairs(m):
    pairs = []
    for l in range(LAYERS):
        for core in range(CORES):
            group = GROUP_OF[m][(l + 2 * core) % LAYERS]
            pairs.append(((l, core), (2 * core + group // CORES, group % CORES)))
    return pairs


def exchanged(block):
    ctx_count, tp_count = lax.axis_size("ctx"), lax.axis_size("tp")
    groups = [
        [c * tp_count + tp for c in range(ctx_count) for tp in range(core, tp_count, CORES)]
        for core in range(CORES)
    ]
    flat = block.reshape(block.shape[0], -1, HEAD_DIM)
    got = lax.all_to_all(
        flat, ("ctx", "tp"), split_axis=0, concat_axis=0, axis_index_groups=groups, tiled=True
    )
    return got.reshape(block.shape)


def cut(block, starts, sizes):
    return lax.dynamic_slice(block, starts, sizes, allow_negative_indices=False)


def shards(query_in, key_in, value_in, doc_ids, stretch_order, out_cot):
    ctx_count = lax.axis_size("ctx")
    layer = lax.axis_index("pipe")
    rows = query_in.shape[1]

    got = exchanged(spread(jnp.concatenate([key_in, value_in]), ctx_count))
    pieces = pieces_of(query_in[0], out_cot[0])
    qc_parts = [sent_over(pieces[m], round_pairs(m)) for m in range(LAYERS)]

    position = stretch_order[lax.axis_index("ctx")]
    block_ids = jnp.arange(ctx_count, dtype=jnp.int32)
    wanted = jnp.maximum(position - REACH + jnp.arange(NEAR, dtype=jnp.int32), 0)
    holder = jnp.sum(
        jnp.where(stretch_order[None, :] == wanted[:, None], block_ids[None, :], 0), axis=1
    )

    def window(distance):
        head = lax.rem(layer + distance, LAYERS) // 2
        return jnp.concatenate(
            [
                cut(got, (holder[j] * TILES, 0, head, 0, 0), (TILES, 2, 1, TILE, HEAD_DIM))
                for j in range(NEAR)
            ]
        ).reshape(NEAR * TILES, 2, TILE, HEAD_DIM)

    mine = [window(0)] + [moved(window(d), d) for d in (1, 3, 2)]
    mine = [mine[0], mine[1], mine[3], mine[2]]
    theirs = [swapped(x) for x in mine]

    offsets = jnp.arange(SPAN, dtype=jnp.int32)
    row_ids = jnp.arange(rows, dtype=jnp.int32)
    documents = jnp.concatenate([jnp.full((REACH * BLOCK,), -1, jnp.int32), doc_ids])
    near_documents = cut(documents, (position * BLOCK,), (SPAN,))
    own_documents = near_documents[REACH * BLOCK:]
    allowed = (offsets[None, :] <= row_ids[:, None] + REACH * BLOCK) & (
        near_documents[None, :] == own_documents[:, None]
    )
    bias = jnp.where(allowed, 0.0, masked_score).astype(f32)

    keep, give, *groups = run_layers(bias, mine, theirs, qc_parts)
    received = swapped(give)
    sums = [
        (keep[d].astype(f32) + received[d].astype(f32)).astype(bf16) for d in range(LAYERS)
    ]
    parts = [sums[0]] + [moved(sums[d], d) for d in (1, 3, 2)]
    parts = [parts[0], parts[1], parts[3], parts[2]]
    grad_key, grad_value = total(exchanged(place(stretch_order, parts)))
    out, grad_query = assemble(
        [
            sent_over(groups[m], [(b, a) for a, b in round_pairs(m)]) for m in range(LAYERS)
        ]
    )
    return (out[None], grad_query[None], grad_key[None], grad_value[None])


def solution(mesh):
    return jax.shard_map(
        shards,
        mesh=mesh,
        in_specs=(
            P("pipe", "ctx", "tp"),
            P("pipe", ("ctx", "tp"), None),
            P("pipe", ("ctx", "tp"), None),
            P(),
            P(),
            P("pipe", "ctx", "tp"),
        ),
        out_specs=(
            P("pipe", "ctx", "tp"),
            P("pipe", "ctx", "tp"),
            P("pipe", ("ctx", "tp"), None),
            P("pipe", ("ctx", "tp"), None),
        ),
        check_vma=False,
    )
```

```python
import math

import jax
import jax.numpy as jnp
from jax import lax
from jax.experimental import pallas as pl
from jax.experimental.pallas import tpu as pltpu
from jax.sharding import PartitionSpec as P

HEAD_DIM = 128
BLOCK = 128
REACH = 4
NEAR = REACH + 1
SPAN = NEAR * BLOCK
LAYERS = 4
TILE = 16
CORES = 2
TILES = BLOCK // TILE // CORES
SCALE = HEAD_DIM ** (-0.5)
EXP2_SCALE = SCALE * math.log2(math.e)

masked_score = -1e30
bf16 = jnp.bfloat16
f32 = jnp.float32
ANY = pl.BlockSpec(memory_space=pl.ANY)
HBM = pl.BlockSpec(memory_space=pltpu.HBM)
VMEM = pl.BlockSpec(memory_space=pltpu.VMEM)
SMEM = pl.BlockSpec(memory_space=pltpu.SMEM)
PARAMS = pltpu.CompilerParams(vmem_limit_bytes=48 * 1024 * 1024)


def shape(*dims, dtype=bf16):
    return jax.ShapeDtypeStruct(dims, dtype)


def nt(a, b):
    return lax.dot_general(a, b, (((1,), (1,)), ((), ())), preferred_element_type=f32)


def nn(a, b):
    return lax.dot_general(a, b, (((1,), (0,)), ((), ())), preferred_element_type=f32)


def run_copies(pairs, sems, meanwhile=None):
    copies = [pltpu.make_async_copy(a, b, sems.at[i]) for i, (a, b) in enumerate(pairs)]
    for copy in copies:
        copy.start()
    if meanwhile is not None:
        meanwhile()
    for copy in copies:
        copy.wait()


def place_of():
    pipe = lax.axis_index("pipe")
    core = lax.rem(lax.axis_index("tp"), CORES)
    return pipe, core, lax.rem(pipe, 2) * CORES + core


def spread_kernel(kv_in, sent, kv, tiles, sem, sems):
    count = tiles.shape[0]
    run_copies([(kv_in, kv)], sem)
    for x in range(count):
        for kind in range(2):
            for j in range(2):
                head = 2 * x + j
                tiles[x, kind, j] = kv[kind, :, head * HEAD_DIM:(head + 1) * HEAD_DIM]
    run_copies(
        [(tiles, sent.at[pl.ds(c * count, count)]) for c in range(sent.shape[0] // count)], sems
    )


def spread(kv, ctx_count):
    return pl.pallas_call(
        spread_kernel,
        out_shape=shape(ctx_count * TILES, 2, 2, TILE, HEAD_DIM),
        in_specs=[ANY],
        out_specs=ANY,
        scratch_shapes=[
            pltpu.VMEM(kv.shape, bf16),
            pltpu.VMEM((TILES, 2, 2, TILE, HEAD_DIM), bf16),
            pltpu.SemaphoreType.DMA((1,)),
            pltpu.SemaphoreType.DMA((ctx_count,)),
        ],
        compiler_params=PARAMS,
        name="spread",
    )(kv)


LAYER_OF = ((1, 2, 0, 3), (3, 0, 1, 2), (2, 1, 3, 0), (0, 3, 2, 1))
GROUP_OF = tuple(tuple(row.index(l) for l in range(LAYERS)) for row in LAYER_OF)


def chosen(row, index):
    value = jnp.int32(row[0])
    for i in range(1, len(row)):
        value = jnp.where(index == i, row[i], value)
    return value


def group_of(m):
    pipe, core, _ = place_of()
    return chosen(GROUP_OF[m], lax.rem(pipe + 2 * core, LAYERS))


def layer_of(m):
    pipe, _, group = place_of()
    return lax.rem(chosen(LAYER_OF[m], group) + 2 * (pipe // 2), LAYERS)


def pieces_kernel(query, cot, p0, p1, p2, p3, sems):
    width = p0.shape[2]
    pairs = []
    for m, piece in enumerate((p0, p1, p2, p3)):
        column = pl.multiple_of(group_of(m) * width, width)
        for i, whole in enumerate((query, cot)):
            pairs.append((whole.at[:, pl.ds(column, width)], piece.at[i]))
    run_copies(pairs, sems)


def pieces_of(query, cot):
    rows, width = query.shape
    return pl.pallas_call(
        pieces_kernel,
        out_shape=(shape(2, rows, width // LAYERS),) * LAYERS,
        in_specs=[HBM, HBM],
        out_specs=(ANY,) * LAYERS,
        scratch_shapes=[pltpu.SemaphoreType.DMA((2 * LAYERS,))],
        compiler_params=PARAMS,
        name="pieces",
    )(query, cot)


def layers_kernel(
    bias_in, a0, a1, a2, a3, b0, b1, b2, b3, q0, q1, q2, q3,
    keep, give, og0, og1, og2, og3,
    bias, kv, qc, og, dkv, expo, queries, scale_rows, gs_all, ds_all, sems, out_sems,
):
    layers, _, rows, width = qc.shape
    heads = width // HEAD_DIM
    pipe, core, group = place_of()

    def back(start, d):
        return lax.rem(start + layers - d, layers)

    pairs = []
    for k in range(2):
        for d, x in enumerate((a0, a1, a2, a3)):
            pairs.append((x.at[:, k], kv.at[k, back(pipe, d), :, core]))
        for d, x in enumerate((b0, b1, b2, b3)):
            pairs.append((x.at[:, k], kv.at[k, back(pipe, d), :, 1 - core]))
    for m, x in enumerate((q0, q1, q2, q3)):
        pairs.append((x, qc.at[layer_of(m)]))
    pairs.append((bias_in, bias))
    run_copies(pairs, sems)

    def cols(h):
        return slice(h * HEAD_DIM, (h + 1) * HEAD_DIM)

    def span(h):
        return slice(h * rows, (h + 1) * rows)

    def keys(l):
        return kv[0, l].reshape(SPAN, HEAD_DIM)

    def values(l):
        return kv[1, l].reshape(SPAN, HEAD_DIM)

    ones = jnp.ones((SPAN, HEAD_DIM), bf16)
    for l in range(layers):
        for h in range(heads):
            q = qc[l, 0, :, cols(h)]
            if l > 0:
                q = (q.astype(f32) + og[l - 1, 0, :, cols(h)].astype(f32)).astype(bf16)
            queries[l, span(h)] = q
            t = nt(q, keys(l)) * EXP2_SCALE + bias[...]
            e = jnp.exp2(t - jnp.max(t, axis=-1, keepdims=True)).astype(bf16)
            expo[l, span(h)] = e
            mixed = nn(e, jnp.concatenate([values(l), ones], axis=1))
            r = 1.0 / mixed[:, HEAD_DIM:]
            scale_rows[l, span(h)] = r
            og[l, 0, :, cols(h)] = (mixed[:, :HEAD_DIM] * r).astype(bf16)

    def probs_grad(l, h):
        g = qc[l, 1, :, cols(h)]
        if l < layers - 1:
            g = (g.astype(f32) + og[l + 1, 1, :, cols(h)].astype(f32)).astype(bf16)
        gs = (g.astype(f32) * scale_rows[l, span(h)]).astype(bf16)
        gs_all[l, span(h)] = gs
        delta = jnp.sum(gs.astype(f32) * og[l, 0, :, cols(h)].astype(f32), axis=-1, keepdims=True)
        return nt(gs, values(l)), delta

    def scores_grad(l, h, dp, delta):
        ds = (expo[l, span(h)].astype(f32) * (dp - delta)).astype(bf16)
        ds_all[l, span(h)] = ds
        return ds

    def query_grad(l, h, ds):
        og[l, 1, :, cols(h)] = (nn(ds, keys(l)) * SCALE).astype(bf16)
        if h == heads - 1:
            gk = nn(queries[l].T, ds_all[l]) * SCALE
            gv = nn(gs_all[l].T, expo[l])
            dkv[0, l] = gk.T.astype(bf16).reshape(NEAR * TILES, CORES, TILE, HEAD_DIM)
            dkv[1, l] = gv.T.astype(bf16).reshape(NEAR * TILES, CORES, TILE, HEAD_DIM)

    steps = [(l, h) for l in reversed(range(layers)) for h in range(heads)]
    first, second = {}, {}
    for i in range(len(steps) + 2):
        if i < len(steps):
            first[i] = probs_grad(*steps[i])
        if 1 <= i <= len(steps):
            second[i - 1] = scores_grad(*steps[i - 1], *first.pop(i - 1))
        if i >= 2:
            query_grad(*steps[i - 2], second.pop(i - 2))

    pairs = []
    for d in range(layers):
        l = lax.rem(pipe + d, layers)
        for k in range(2):
            pairs.append((dkv.at[k, l, :, 1 - core], give.at[d, k]))
            pairs.append((dkv.at[k, l, :, core], keep.at[d, k]))
    for m, x in enumerate((og0, og1, og2, og3)):
        pairs.append((og.at[layer_of(m)], x))
    run_copies(pairs, out_sems)


def run_layers(bias, mine, theirs, qc_parts):
    _, rows, width = qc_parts[0].shape
    stacked = rows * width // HEAD_DIM
    kv_shape = shape(LAYERS, 2, NEAR * TILES, TILE, HEAD_DIM)
    return pl.pallas_call(
        layers_kernel,
        out_shape=(kv_shape, kv_shape) + (shape(2, rows, width),) * LAYERS,
        in_specs=[ANY] * 13,
        out_specs=(ANY,) * 6,
        scratch_shapes=[
            pltpu.VMEM((rows, SPAN), f32),
            pltpu.VMEM((2, LAYERS, NEAR * TILES, CORES, TILE, HEAD_DIM), bf16),
            pltpu.VMEM((LAYERS, 2, rows, width), bf16),
            pltpu.VMEM((LAYERS, 2, rows, width), bf16),
            pltpu.VMEM((2, LAYERS, NEAR * TILES, CORES, TILE, HEAD_DIM), bf16),
            pltpu.VMEM((LAYERS, stacked, SPAN), bf16),
            pltpu.VMEM((LAYERS, stacked, HEAD_DIM), bf16),
            pltpu.VMEM((LAYERS, stacked, HEAD_DIM), f32),
            pltpu.VMEM((LAYERS, stacked, HEAD_DIM), bf16),
            pltpu.VMEM((LAYERS, stacked, SPAN), bf16),
            pltpu.SemaphoreType.DMA((21,)),
            pltpu.SemaphoreType.DMA((20,)),
        ],
        compiler_params=PARAMS,
        name="layers",
    )(bias, *mine, *theirs, *qc_parts)


def place_kernel(order_in, p0, p1, p2, p3, sent_out, order, parts, sent, sems, out_sems):
    pipe, _, _ = place_of()

    def clear():
        sent[...] = jnp.zeros(sent.shape, bf16)

    run_copies(
        [(order_in, order)]
        + [
            (x, parts.at[lax.rem(pipe + LAYERS - d, LAYERS)])
            for d, x in enumerate((p0, p1, p2, p3))
        ],
        sems,
        clear,
    )
    first = order[lax.axis_index("ctx")] - REACH
    for c in range(sent.shape[1]):
        j = order[c] - first

        @pl.when((j >= 0) & (j <= REACH))
        def _():
            at = pl.ds(j * TILES, TILES)
            for head in range(2):
                total = parts[2 * head, :, at].astype(f32) + parts[2 * head + 1, :, at].astype(f32)
                total = total.astype(bf16)
                for k in range(2):
                    sent[:, c, k, head] = total[k]

    run_copies([(sent, sent_out)], out_sems)


def place(order, parts):
    return pl.pallas_call(
        place_kernel,
        out_shape=shape(TILES, order.shape[0], 2, 2, TILE, HEAD_DIM),
        in_specs=[ANY] * (1 + LAYERS),
        out_specs=ANY,
        scratch_shapes=[
            pltpu.SMEM(order.shape, jnp.int32),
            pltpu.VMEM((LAYERS,) + parts[0].shape, bf16),
            pltpu.VMEM((TILES, order.shape[0], 2, 2, TILE, HEAD_DIM), bf16),
            pltpu.SemaphoreType.DMA((1 + LAYERS,)),
            pltpu.SemaphoreType.DMA((1,)),
        ],
        compiler_params=PARAMS,
        name="place",
    )(order, *parts)


def total_kernel(got_in, grad_key, grad_value, got, sem):
    copy = pltpu.make_async_copy(got_in, got, sem)
    copy.start()
    copy.wait()
    for x in range(TILES):
        total = got[x, 0].astype(f32)
        for c in range(1, got.shape[1]):
            total = total + got[x, c].astype(f32)
        total = total.astype(bf16)
        for kind, whole in enumerate((grad_key, grad_value)):
            for j in range(2):
                head = 2 * x + j
                whole[:, head * HEAD_DIM:(head + 1) * HEAD_DIM] = total[kind, j]


def total(got):
    return pl.pallas_call(
        total_kernel,
        out_shape=(shape(TILE, TILES * 2 * HEAD_DIM),) * 2,
        in_specs=[ANY],
        out_specs=(VMEM, VMEM),
        scratch_shapes=[pltpu.VMEM(got.shape, bf16), pltpu.SemaphoreType.DMA],
        compiler_params=PARAMS,
        name="total",
    )(got)


def assemble_kernel(g0, g1, g2, g3, out, grad_query, sems):
    width = g0.shape[2]
    pairs = []
    for m, piece in enumerate((g0, g1, g2, g3)):
        column = pl.multiple_of(group_of(m) * width, width)
        for i, whole in enumerate((out, grad_query)):
            pairs.append((piece.at[i], whole.at[:, pl.ds(column, width)]))
    run_copies(pairs, sems)


def assemble(pieces):
    _, rows, width = pieces[0].shape
    return pl.pallas_call(
        assemble_kernel,
        out_shape=(shape(rows, LAYERS * width),) * 2,
        in_specs=[ANY] * 4,
        out_specs=(ANY, ANY),
        scratch_shapes=[pltpu.SemaphoreType.DMA((8,))],
        compiler_params=PARAMS,
        name="assemble",
    )(*pieces)


def moved(block, distance):
    size = lax.axis_size("pipe")
    return lax.ppermute(block, "pipe", [(i, (i + distance) % size) for i in range(size)])


def swapped(block):
    size = lax.axis_size("tp")
    return lax.ppermute(block, "tp", [(i, i ^ 1) for i in range(size)])


def sent_over(block, pairs):
    tp_count = lax.axis_size("tp")
    route = [
        (a * tp_count + x + b, c * tp_count + x + d)
        for (a, b), (c, d) in pairs
        for x in range(0, tp_count, CORES)
    ]
    return lax.ppermute(block, ("pipe", "tp"), route)


def round_pairs(m):
    pairs = []
    for l in range(LAYERS):
        for core in range(CORES):
            group = GROUP_OF[m][(l + 2 * core) % LAYERS]
            pairs.append(((l, core), (2 * core + group // CORES, group % CORES)))
    return pairs


def exchanged(block):
    ctx_count, tp_count = lax.axis_size("ctx"), lax.axis_size("tp")
    groups = [
        [c * tp_count + tp for c in range(ctx_count) for tp in range(core, tp_count, CORES)]
        for core in range(CORES)
    ]
    flat = block.reshape(TILES * ctx_count, -1, HEAD_DIM)
    got = lax.all_to_all(
        flat, ("ctx", "tp"), split_axis=0, concat_axis=0, axis_index_groups=groups, tiled=True
    )
    return got.reshape(block.shape)


def exchanged_by_x(block):
    ctx_count, tp_count = lax.axis_size("ctx"), lax.axis_size("tp")
    groups = [
        [c * tp_count + tp for tp in range(core, tp_count, CORES) for c in range(ctx_count)]
        for core in range(CORES)
    ]
    flat = block.reshape(TILES * ctx_count, -1, HEAD_DIM)
    got = lax.all_to_all(
        flat, ("ctx", "tp"), split_axis=0, concat_axis=0, axis_index_groups=groups, tiled=True
    )
    return got.reshape(block.shape)


def cut(block, starts, sizes):
    return lax.dynamic_slice(block, starts, sizes, allow_negative_indices=False)


def shards(query_in, key_in, value_in, doc_ids, stretch_order, out_cot):
    ctx_count = lax.axis_size("ctx")
    layer = lax.axis_index("pipe")
    rows = query_in.shape[1]

    got = exchanged(spread(jnp.concatenate([key_in, value_in]), ctx_count))
    pieces = pieces_of(query_in[0], out_cot[0])
    qc_parts = [sent_over(pieces[m], round_pairs(m)) for m in range(LAYERS)]

    position = stretch_order[lax.axis_index("ctx")]
    block_ids = jnp.arange(ctx_count, dtype=jnp.int32)
    wanted = jnp.maximum(position - REACH + jnp.arange(NEAR, dtype=jnp.int32), 0)
    holder = jnp.sum(
        jnp.where(stretch_order[None, :] == wanted[:, None], block_ids[None, :], 0), axis=1
    )

    def window(distance):
        head = lax.rem(layer + distance, LAYERS) // 2
        return jnp.concatenate(
            [
                cut(got, (holder[j] * TILES, 0, head, 0, 0), (TILES, 2, 1, TILE, HEAD_DIM))
                for j in range(NEAR)
            ]
        ).reshape(NEAR * TILES, 2, TILE, HEAD_DIM)

    mine = [window(0)] + [moved(window(d), d) for d in (1, 3, 2)]
    mine = [mine[0], mine[1], mine[3], mine[2]]
    theirs = [swapped(x) for x in mine]

    offsets = jnp.arange(SPAN, dtype=jnp.int32)
    row_ids = jnp.arange(rows, dtype=jnp.int32)
    documents = jnp.concatenate([jnp.full((REACH * BLOCK,), -1, jnp.int32), doc_ids])
    near_documents = cut(documents, (position * BLOCK,), (SPAN,))
    own_documents = near_documents[REACH * BLOCK:]
    allowed = (offsets[None, :] <= row_ids[:, None] + REACH * BLOCK) & (
        near_documents[None, :] == own_documents[:, None]
    )
    bias = jnp.where(allowed, 0.0, masked_score).astype(f32)

    keep, give, *groups = run_layers(bias, mine, theirs, qc_parts)
    received = swapped(give)
    sums = [
        (keep[d].astype(f32) + received[d].astype(f32)).astype(bf16) for d in range(LAYERS)
    ]
    parts = [sums[0]] + [moved(sums[d], d) for d in (1, 3, 2)]
    parts = [parts[0], parts[1], parts[3], parts[2]]
    grad_key, grad_value = total(exchanged_by_x(place(stretch_order, parts)))
    out, grad_query = assemble(
        [
            sent_over(groups[m], [(b, a) for a, b in round_pairs(m)]) for m in range(LAYERS)
        ]
    )
    return (out[None], grad_query[None], grad_key[None], grad_value[None])


def solution(mesh):
    return jax.shard_map(
        shards,
        mesh=mesh,
        in_specs=(
            P("pipe", "ctx", "tp"),
            P("pipe", ("ctx", "tp"), None),
            P("pipe", ("ctx", "tp"), None),
            P(),
            P(),
            P("pipe", "ctx", "tp"),
        ),
        out_specs=(
            P("pipe", "ctx", "tp"),
            P("pipe", "ctx", "tp"),
            P("pipe", ("ctx", "tp"), None),
            P("pipe", ("ctx", "tp"), None),
        ),
        check_vma=False,
    )
```

```python
import math

import jax
import jax.numpy as jnp
from jax import lax
from jax.experimental import pallas as pl
from jax.experimental.pallas import tpu as pltpu
from jax.sharding import PartitionSpec as P

HEAD_DIM = 128
BLOCK = 128
REACH = 4
NEAR = REACH + 1
SPAN = NEAR * BLOCK
LAYERS = 4
TILE = 16
CORES = 2
TILES = BLOCK // TILE // CORES
SCALE = HEAD_DIM ** (-0.5)
EXP2_SCALE = SCALE * math.log2(math.e)

masked_score = -1e30
bf16 = jnp.bfloat16
f32 = jnp.float32
ANY = pl.BlockSpec(memory_space=pl.ANY)
HBM = pl.BlockSpec(memory_space=pltpu.HBM)
VMEM = pl.BlockSpec(memory_space=pltpu.VMEM)
SMEM = pl.BlockSpec(memory_space=pltpu.SMEM)
PARAMS = pltpu.CompilerParams(vmem_limit_bytes=48 * 1024 * 1024)


def shape(*dims, dtype=bf16):
    return jax.ShapeDtypeStruct(dims, dtype)


def nt(a, b):
    return lax.dot_general(a, b, (((1,), (1,)), ((), ())), preferred_element_type=f32)


def nn(a, b):
    return lax.dot_general(a, b, (((1,), (0,)), ((), ())), preferred_element_type=f32)


def run_copies(pairs, sems, meanwhile=None):
    copies = [pltpu.make_async_copy(a, b, sems.at[i]) for i, (a, b) in enumerate(pairs)]
    for copy in copies:
        copy.start()
    if meanwhile is not None:
        meanwhile()
    for copy in copies:
        copy.wait()


def place_of():
    pipe = lax.axis_index("pipe")
    core = lax.rem(lax.axis_index("tp"), CORES)
    return pipe, core, lax.rem(pipe, 2) * CORES + core


def spread_kernel(kv_in, sent, kv, tiles, sem, sems):
    count = tiles.shape[0]
    run_copies([(kv_in, kv)], sem)
    for x in range(count):
        for kind in range(2):
            for j in range(2):
                head = 2 * x + j
                tiles[x, kind, j] = kv[kind, :, head * HEAD_DIM:(head + 1) * HEAD_DIM]
    run_copies(
        [(tiles, sent.at[pl.ds(c * count, count)]) for c in range(sent.shape[0] // count)], sems
    )


def spread(kv, ctx_count):
    return pl.pallas_call(
        spread_kernel,
        out_shape=shape(ctx_count * TILES, 2, 2, TILE, HEAD_DIM),
        in_specs=[ANY],
        out_specs=ANY,
        scratch_shapes=[
            pltpu.VMEM(kv.shape, bf16),
            pltpu.VMEM((TILES, 2, 2, TILE, HEAD_DIM), bf16),
            pltpu.SemaphoreType.DMA((1,)),
            pltpu.SemaphoreType.DMA((ctx_count,)),
        ],
        compiler_params=PARAMS,
        name="spread",
    )(kv)


LAYER_OF = ((1, 2, 0, 3), (3, 0, 1, 2), (2, 1, 3, 0), (0, 3, 2, 1))
GROUP_OF = tuple(tuple(row.index(l) for l in range(LAYERS)) for row in LAYER_OF)


def chosen(row, index):
    value = jnp.int32(row[0])
    for i in range(1, len(row)):
        value = jnp.where(index == i, row[i], value)
    return value


def group_of(m):
    pipe, core, _ = place_of()
    return chosen(GROUP_OF[m], lax.rem(pipe + 2 * core, LAYERS))


def layer_of(m):
    pipe, _, group = place_of()
    return lax.rem(chosen(LAYER_OF[m], group) + 2 * (pipe // 2), LAYERS)


def pieces_kernel(query, cot, p0, p1, p2, p3, sems):
    width = p0.shape[2]
    pairs = []
    for m, piece in enumerate((p0, p1, p2, p3)):
        column = pl.multiple_of(group_of(m) * width, width)
        for i, whole in enumerate((query, cot)):
            pairs.append((whole.at[:, pl.ds(column, width)], piece.at[i]))
    run_copies(pairs, sems)


def pieces_of(query, cot):
    rows, width = query.shape
    return pl.pallas_call(
        pieces_kernel,
        out_shape=(shape(2, rows, width // LAYERS),) * LAYERS,
        in_specs=[HBM, HBM],
        out_specs=(ANY,) * LAYERS,
        scratch_shapes=[pltpu.SemaphoreType.DMA((2 * LAYERS,))],
        compiler_params=PARAMS,
        name="pieces",
    )(query, cot)


def layers_kernel(
    bias_in, a0, a1, a2, a3, b0, b1, b2, b3, q0, q1, q2, q3,
    keep, give, og0, og1, og2, og3,
    bias, kv, qc, og, dkv, expo, queries, scale_rows, gs_all, ds_all, sems, out_sems,
):
    layers, _, rows, width = qc.shape
    heads = width // HEAD_DIM
    pipe, core, group = place_of()

    def back(start, d):
        return lax.rem(start + layers - d, layers)

    pairs = []
    for k in range(2):
        for d, x in enumerate((a0, a1, a2, a3)):
            pairs.append((x.at[:, k], kv.at[k, back(pipe, d), :, core]))
        for d, x in enumerate((b0, b1, b2, b3)):
            pairs.append((x.at[:, k], kv.at[k, back(pipe, d), :, 1 - core]))
    for m, x in enumerate((q0, q1, q2, q3)):
        pairs.append((x, qc.at[layer_of(m)]))
    pairs.append((bias_in, bias))
    run_copies(pairs, sems)

    def cols(h):
        return slice(h * HEAD_DIM, (h + 1) * HEAD_DIM)

    def span(h):
        return slice(h * rows, (h + 1) * rows)

    def keys(l):
        return kv[0, l].reshape(SPAN, HEAD_DIM)

    def values(l):
        return kv[1, l].reshape(SPAN, HEAD_DIM)

    ones = jnp.ones((SPAN, HEAD_DIM), bf16)
    for l in range(layers):
        for h in range(heads):
            q = qc[l, 0, :, cols(h)]
            if l > 0:
                q = (q.astype(f32) + og[l - 1, 0, :, cols(h)].astype(f32)).astype(bf16)
            queries[l, span(h)] = q
            t = nt(q, keys(l)) * EXP2_SCALE + bias[...]
            e = jnp.exp2(t - jnp.max(t, axis=-1, keepdims=True)).astype(bf16)
            expo[l, span(h)] = e
            mixed = nn(e, jnp.concatenate([values(l), ones], axis=1))
            r = 1.0 / mixed[:, HEAD_DIM:]
            scale_rows[l, span(h)] = r
            og[l, 0, :, cols(h)] = (mixed[:, :HEAD_DIM] * r).astype(bf16)

    def probs_grad(l, h):
        g = qc[l, 1, :, cols(h)]
        if l < layers - 1:
            g = (g.astype(f32) + og[l + 1, 1, :, cols(h)].astype(f32)).astype(bf16)
        gs = (g.astype(f32) * scale_rows[l, span(h)]).astype(bf16)
        gs_all[l, span(h)] = gs
        delta = jnp.sum(gs.astype(f32) * og[l, 0, :, cols(h)].astype(f32), axis=-1, keepdims=True)
        return nt(gs, values(l)), delta

    def scores_grad(l, h, dp, delta):
        ds = (expo[l, span(h)].astype(f32) * (dp - delta)).astype(bf16)
        ds_all[l, span(h)] = ds
        return ds

    def query_grad(l, h, ds):
        og[l, 1, :, cols(h)] = (nn(ds, keys(l)) * SCALE).astype(bf16)
        if h == heads - 1:
            gk = nn(queries[l].T, ds_all[l]) * SCALE
            gv = nn(gs_all[l].T, expo[l])
            dkv[0, l] = gk.T.astype(bf16).reshape(NEAR * TILES, CORES, TILE, HEAD_DIM)
            dkv[1, l] = gv.T.astype(bf16).reshape(NEAR * TILES, CORES, TILE, HEAD_DIM)

    steps = [(l, h) for l in reversed(range(layers)) for h in range(heads)]
    first, second = {}, {}
    for i in range(len(steps) + 2):
        if i < len(steps):
            first[i] = probs_grad(*steps[i])
        if 1 <= i <= len(steps):
            second[i - 1] = scores_grad(*steps[i - 1], *first.pop(i - 1))
        if i >= 2:
            query_grad(*steps[i - 2], second.pop(i - 2))

    pairs = []
    for d in range(layers):
        l = lax.rem(pipe + d, layers)
        for k in range(2):
            pairs.append((dkv.at[k, l, :, 1 - core], give.at[d, k]))
            pairs.append((dkv.at[k, l, :, core], keep.at[d, k]))
    for m, x in enumerate((og0, og1, og2, og3)):
        pairs.append((og.at[layer_of(m)], x))
    run_copies(pairs, out_sems)


def run_layers(bias, mine, theirs, qc_parts):
    _, rows, width = qc_parts[0].shape
    stacked = rows * width // HEAD_DIM
    kv_shape = shape(LAYERS, 2, NEAR * TILES, TILE, HEAD_DIM)
    return pl.pallas_call(
        layers_kernel,
        out_shape=(kv_shape, kv_shape) + (shape(2, rows, width),) * LAYERS,
        in_specs=[ANY] * 13,
        out_specs=(ANY,) * 6,
        scratch_shapes=[
            pltpu.VMEM((rows, SPAN), f32),
            pltpu.VMEM((2, LAYERS, NEAR * TILES, CORES, TILE, HEAD_DIM), bf16),
            pltpu.VMEM((LAYERS, 2, rows, width), bf16),
            pltpu.VMEM((LAYERS, 2, rows, width), bf16),
            pltpu.VMEM((2, LAYERS, NEAR * TILES, CORES, TILE, HEAD_DIM), bf16),
            pltpu.VMEM((LAYERS, stacked, SPAN), bf16),
            pltpu.VMEM((LAYERS, stacked, HEAD_DIM), bf16),
            pltpu.VMEM((LAYERS, stacked, HEAD_DIM), f32),
            pltpu.VMEM((LAYERS, stacked, HEAD_DIM), bf16),
            pltpu.VMEM((LAYERS, stacked, SPAN), bf16),
            pltpu.SemaphoreType.DMA((21,)),
            pltpu.SemaphoreType.DMA((20,)),
        ],
        compiler_params=PARAMS,
        name="layers",
    )(bias, *mine, *theirs, *qc_parts)


def place_kernel(
    order_in, p0, p1, p2, p3, sent_out, order, parts, sent, order_sem, sems, out_sems
):
    pipe, _, _ = place_of()
    order_copy = pltpu.make_async_copy(order_in, order, order_sem)
    order_copy.start()
    copies = [
        pltpu.make_async_copy(
            x, parts.at[lax.rem(pipe + LAYERS - d, LAYERS)], sems.at[d]
        )
        for d, x in enumerate((p0, p1, p2, p3))
    ]
    for copy in copies:
        copy.start()
    sent[...] = jnp.zeros(sent.shape, bf16)
    order_copy.wait()
    first = order[lax.axis_index("ctx")] - REACH
    outs = [
        pltpu.make_async_copy(sent.at[:, c], sent_out.at[:, c], out_sems.at[c])
        for c in range(sent.shape[1])
    ]
    steps = [order[c] - first for c in range(sent.shape[1])]
    nears = [(j >= 0) & (j <= REACH) for j in steps]
    for near, out in zip(nears, outs):

        @pl.when(jnp.logical_not(near))
        def _(out=out):
            out.start()

    for copy in copies:
        copy.wait()
    for c, (j, near, out) in enumerate(zip(steps, nears, outs)):

        @pl.when(near)
        def _(c=c, j=j, out=out):
            at = pl.ds(j * TILES, TILES)
            for head in range(2):
                total = parts[2 * head, :, at].astype(f32) + parts[2 * head + 1, :, at].astype(f32)
                total = total.astype(bf16)
                for k in range(2):
                    sent[:, c, k, head] = total[k]
            out.start()

    for out in outs:
        out.wait()


def place(order, parts):
    return pl.pallas_call(
        place_kernel,
        out_shape=shape(TILES, order.shape[0], 2, 2, TILE, HEAD_DIM),
        in_specs=[ANY] * (1 + LAYERS),
        out_specs=ANY,
        scratch_shapes=[
            pltpu.SMEM(order.shape, jnp.int32),
            pltpu.VMEM((LAYERS,) + parts[0].shape, bf16),
            pltpu.VMEM((TILES, order.shape[0], 2, 2, TILE, HEAD_DIM), bf16),
            pltpu.SemaphoreType.DMA,
            pltpu.SemaphoreType.DMA((LAYERS,)),
            pltpu.SemaphoreType.DMA(order.shape),
        ],
        compiler_params=PARAMS,
        name="place",
    )(order, *parts)


def total_kernel(got_in, grad_key, grad_value, got, sem):
    copy = pltpu.make_async_copy(got_in, got, sem)
    copy.start()
    copy.wait()
    for x in range(TILES):
        total = got[x, 0].astype(f32)
        for c in range(1, got.shape[1]):
            total = total + got[x, c].astype(f32)
        total = total.astype(bf16)
        for kind, whole in enumerate((grad_key, grad_value)):
            for j in range(2):
                head = 2 * x + j
                whole[:, head * HEAD_DIM:(head + 1) * HEAD_DIM] = total[kind, j]


def total(got):
    return pl.pallas_call(
        total_kernel,
        out_shape=(shape(TILE, TILES * 2 * HEAD_DIM),) * 2,
        in_specs=[ANY],
        out_specs=(VMEM, VMEM),
        scratch_shapes=[pltpu.VMEM(got.shape, bf16), pltpu.SemaphoreType.DMA],
        compiler_params=PARAMS,
        name="total",
    )(got)


def assemble_kernel(g0, g1, g2, g3, out, grad_query, sems):
    width = g0.shape[2]
    pairs = []
    for m, piece in enumerate((g0, g1, g2, g3)):
        column = pl.multiple_of(group_of(m) * width, width)
        for i, whole in enumerate((out, grad_query)):
            pairs.append((piece.at[i], whole.at[:, pl.ds(column, width)]))
    run_copies(pairs, sems)


def assemble(pieces):
    _, rows, width = pieces[0].shape
    return pl.pallas_call(
        assemble_kernel,
        out_shape=(shape(rows, LAYERS * width),) * 2,
        in_specs=[ANY] * 4,
        out_specs=(ANY, ANY),
        scratch_shapes=[pltpu.SemaphoreType.DMA((8,))],
        compiler_params=PARAMS,
        name="assemble",
    )(*pieces)


def moved(block, distance):
    size = lax.axis_size("pipe")
    return lax.ppermute(block, "pipe", [(i, (i + distance) % size) for i in range(size)])


def swapped(block):
    size = lax.axis_size("tp")
    return lax.ppermute(block, "tp", [(i, i ^ 1) for i in range(size)])


def sent_over(block, pairs):
    tp_count = lax.axis_size("tp")
    route = [
        (a * tp_count + x + b, c * tp_count + x + d)
        for (a, b), (c, d) in pairs
        for x in range(0, tp_count, CORES)
    ]
    return lax.ppermute(block, ("pipe", "tp"), route)


def round_pairs(m):
    pairs = []
    for l in range(LAYERS):
        for core in range(CORES):
            group = GROUP_OF[m][(l + 2 * core) % LAYERS]
            pairs.append(((l, core), (2 * core + group // CORES, group % CORES)))
    return pairs


def exchanged(block):
    ctx_count, tp_count = lax.axis_size("ctx"), lax.axis_size("tp")
    groups = [
        [c * tp_count + tp for c in range(ctx_count) for tp in range(core, tp_count, CORES)]
        for core in range(CORES)
    ]
    flat = block.reshape(TILES * ctx_count, -1, HEAD_DIM)
    got = lax.all_to_all(
        flat, ("ctx", "tp"), split_axis=0, concat_axis=0, axis_index_groups=groups, tiled=True
    )
    return got.reshape(block.shape)


def exchanged_by_x(block):
    ctx_count, tp_count = lax.axis_size("ctx"), lax.axis_size("tp")
    groups = [
        [c * tp_count + tp for tp in range(core, tp_count, CORES) for c in range(ctx_count)]
        for core in range(CORES)
    ]
    flat = block.reshape(TILES * ctx_count, -1, HEAD_DIM)
    got = lax.all_to_all(
        flat, ("ctx", "tp"), split_axis=0, concat_axis=0, axis_index_groups=groups, tiled=True
    )
    return got.reshape(block.shape)


def cut(block, starts, sizes):
    return lax.dynamic_slice(block, starts, sizes, allow_negative_indices=False)


def shards(query_in, key_in, value_in, doc_ids, stretch_order, out_cot):
    ctx_count = lax.axis_size("ctx")
    layer = lax.axis_index("pipe")
    rows = query_in.shape[1]

    got = exchanged(spread(jnp.concatenate([key_in, value_in]), ctx_count))
    pieces = pieces_of(query_in[0], out_cot[0])
    qc_parts = [sent_over(pieces[m], round_pairs(m)) for m in range(LAYERS)]

    position = stretch_order[lax.axis_index("ctx")]
    block_ids = jnp.arange(ctx_count, dtype=jnp.int32)
    wanted = jnp.maximum(position - REACH + jnp.arange(NEAR, dtype=jnp.int32), 0)
    holder = jnp.sum(
        jnp.where(stretch_order[None, :] == wanted[:, None], block_ids[None, :], 0), axis=1
    )

    def window(distance):
        head = lax.rem(layer + distance, LAYERS) // 2
        return jnp.concatenate(
            [
                cut(got, (holder[j] * TILES, 0, head, 0, 0), (TILES, 2, 1, TILE, HEAD_DIM))
                for j in range(NEAR)
            ]
        ).reshape(NEAR * TILES, 2, TILE, HEAD_DIM)

    mine = [window(0)] + [moved(window(d), d) for d in (1, 3, 2)]
    mine = [mine[0], mine[1], mine[3], mine[2]]
    theirs = [swapped(x) for x in mine]

    offsets = jnp.arange(SPAN, dtype=jnp.int32)
    row_ids = jnp.arange(rows, dtype=jnp.int32)
    documents = jnp.concatenate([jnp.full((REACH * BLOCK,), -1, jnp.int32), doc_ids])
    near_documents = cut(documents, (position * BLOCK,), (SPAN,))
    own_documents = near_documents[REACH * BLOCK:]
    allowed = (offsets[None, :] <= row_ids[:, None] + REACH * BLOCK) & (
        near_documents[None, :] == own_documents[:, None]
    )
    bias = jnp.where(allowed, 0.0, masked_score).astype(f32)

    keep, give, *groups = run_layers(bias, mine, theirs, qc_parts)
    received = swapped(give)
    sums = [
        (keep[d].astype(f32) + received[d].astype(f32)).astype(bf16) for d in range(LAYERS)
    ]
    parts = [sums[0]] + [moved(sums[d], d) for d in (1, 3, 2)]
    parts = [parts[0], parts[1], parts[3], parts[2]]
    grad_key, grad_value = total(exchanged_by_x(place(stretch_order, parts)))
    out, grad_query = assemble(
        [
            sent_over(groups[m], [(b, a) for a, b in round_pairs(m)]) for m in range(LAYERS)
        ]
    )
    return (out[None], grad_query[None], grad_key[None], grad_value[None])


def solution(mesh):
    return jax.shard_map(
        shards,
        mesh=mesh,
        in_specs=(
            P("pipe", "ctx", "tp"),
            P("pipe", ("ctx", "tp"), None),
            P("pipe", ("ctx", "tp"), None),
            P(),
            P(),
            P("pipe", "ctx", "tp"),
        ),
        out_specs=(
            P("pipe", "ctx", "tp"),
            P("pipe", "ctx", "tp"),
            P("pipe", ("ctx", "tp"), None),
            P("pipe", ("ctx", "tp"), None),
        ),
        check_vma=False,
    )
```

```python
import math

import jax
import jax.numpy as jnp
from jax import lax
from jax.experimental import pallas as pl
from jax.experimental.pallas import tpu as pltpu
from jax.sharding import PartitionSpec as P

HEAD_DIM = 128
BLOCK = 128
REACH = 4
NEAR = REACH + 1
SPAN = NEAR * BLOCK
LAYERS = 4
TILE = 16
CORES = 2
TILES = BLOCK // TILE // CORES
SCALE = HEAD_DIM ** (-0.5)
EXP2_SCALE = SCALE * math.log2(math.e)

masked_score = -1e30
bf16 = jnp.bfloat16
f32 = jnp.float32
ANY = pl.BlockSpec(memory_space=pl.ANY)
HBM = pl.BlockSpec(memory_space=pltpu.HBM)
VMEM = pl.BlockSpec(memory_space=pltpu.VMEM)
SMEM = pl.BlockSpec(memory_space=pltpu.SMEM)
PARAMS = pltpu.CompilerParams(vmem_limit_bytes=48 * 1024 * 1024)


def shape(*dims, dtype=bf16):
    return jax.ShapeDtypeStruct(dims, dtype)


def nt(a, b):
    return lax.dot_general(a, b, (((1,), (1,)), ((), ())), preferred_element_type=f32)


def nn(a, b):
    return lax.dot_general(a, b, (((1,), (0,)), ((), ())), preferred_element_type=f32)


def run_copies(pairs, sems, meanwhile=None):
    copies = [pltpu.make_async_copy(a, b, sems.at[i]) for i, (a, b) in enumerate(pairs)]
    for copy in copies:
        copy.start()
    if meanwhile is not None:
        meanwhile()
    for copy in copies:
        copy.wait()


def place_of():
    pipe = lax.axis_index("pipe")
    core = lax.rem(lax.axis_index("tp"), CORES)
    return pipe, core, lax.rem(pipe, 2) * CORES + core


def spread_kernel(kv_in, sent, kv, tiles, sem, sems):
    count = tiles.shape[0]
    run_copies([(kv_in, kv)], sem)
    for x in range(count):
        for kind in range(2):
            for j in range(2):
                head = 2 * x + j
                tiles[x, kind, j] = kv[kind, :, head * HEAD_DIM:(head + 1) * HEAD_DIM]
    run_copies(
        [(tiles, sent.at[pl.ds(c * count, count)]) for c in range(sent.shape[0] // count)], sems
    )


def spread(kv, ctx_count):
    return pl.pallas_call(
        spread_kernel,
        out_shape=shape(ctx_count * TILES, 2, 2, TILE, HEAD_DIM),
        in_specs=[ANY],
        out_specs=ANY,
        scratch_shapes=[
            pltpu.VMEM(kv.shape, bf16),
            pltpu.VMEM((TILES, 2, 2, TILE, HEAD_DIM), bf16),
            pltpu.SemaphoreType.DMA((1,)),
            pltpu.SemaphoreType.DMA((ctx_count,)),
        ],
        compiler_params=PARAMS,
        name="spread",
    )(kv)


LAYER_OF = ((1, 2, 0, 3), (3, 0, 1, 2), (2, 1, 3, 0), (0, 3, 2, 1))
GROUP_OF = tuple(tuple(row.index(l) for l in range(LAYERS)) for row in LAYER_OF)


def chosen(row, index):
    value = jnp.int32(row[0])
    for i in range(1, len(row)):
        value = jnp.where(index == i, row[i], value)
    return value


def group_of(m):
    pipe, core, _ = place_of()
    return chosen(GROUP_OF[m], lax.rem(pipe + 2 * core, LAYERS))


def layer_of(m):
    pipe, _, group = place_of()
    return lax.rem(chosen(LAYER_OF[m], group) + 2 * (pipe // 2), LAYERS)


def pieces_kernel(query, cot, p0, p1, p2, p3, sems):
    width = p0.shape[2]
    pairs = []
    for m, piece in enumerate((p0, p1, p2, p3)):
        column = pl.multiple_of(group_of(m) * width, width)
        for i, whole in enumerate((query, cot)):
            pairs.append((whole.at[:, pl.ds(column, width)], piece.at[i]))
    run_copies(pairs, sems)


def pieces_of(query, cot):
    rows, width = query.shape
    return pl.pallas_call(
        pieces_kernel,
        out_shape=(shape(2, rows, width // LAYERS),) * LAYERS,
        in_specs=[HBM, HBM],
        out_specs=(ANY,) * LAYERS,
        scratch_shapes=[pltpu.SemaphoreType.DMA((2 * LAYERS,))],
        compiler_params=PARAMS,
        name="pieces",
    )(query, cot)


def layers_kernel(
    bias_in, a0, a1, a2, a3, b0, b1, b2, b3, q0, q1, q2, q3,
    keep, give, og0, og1, og2, og3,
    bias, kv, qc, og, dkv, expo, queries, scale_rows, gs_all, ds_all, sems, out_sems,
):
    layers, _, rows, width = qc.shape
    heads = width // HEAD_DIM
    pipe, core, group = place_of()

    def back(start, d):
        return lax.rem(start + layers - d, layers)

    pairs = []
    for k in range(2):
        for d, x in enumerate((a0, a1, a2, a3)):
            pairs.append((x.at[:, k], kv.at[k, back(pipe, d), :, core]))
        for d, x in enumerate((b0, b1, b2, b3)):
            pairs.append((x.at[:, k], kv.at[k, back(pipe, d), :, 1 - core]))
    for m, x in enumerate((q0, q1, q2, q3)):
        pairs.append((x, qc.at[layer_of(m)]))
    pairs.append((bias_in, bias))
    run_copies(pairs, sems)

    def cols(h):
        return slice(h * HEAD_DIM, (h + 1) * HEAD_DIM)

    def span(h):
        return slice(h * rows, (h + 1) * rows)

    def keys(l):
        return kv[0, l].reshape(SPAN, HEAD_DIM)

    def values(l):
        return kv[1, l].reshape(SPAN, HEAD_DIM)

    ones = jnp.ones((SPAN, HEAD_DIM), bf16)
    for l in range(layers):
        for h in range(heads):
            q = qc[l, 0, :, cols(h)]
            if l > 0:
                q = (q.astype(f32) + og[l - 1, 0, :, cols(h)].astype(f32)).astype(bf16)
            queries[l, span(h)] = q
            t = nt(q, keys(l)) * EXP2_SCALE + bias[...]
            e = jnp.exp2(t - jnp.max(t, axis=-1, keepdims=True)).astype(bf16)
            expo[l, span(h)] = e
            mixed = nn(e, jnp.concatenate([values(l), ones], axis=1))
            r = 1.0 / mixed[:, HEAD_DIM:]
            scale_rows[l, span(h)] = r
            og[l, 0, :, cols(h)] = (mixed[:, :HEAD_DIM] * r).astype(bf16)

    def probs_grad(l, h):
        g = qc[l, 1, :, cols(h)]
        if l < layers - 1:
            g = (g.astype(f32) + og[l + 1, 1, :, cols(h)].astype(f32)).astype(bf16)
        gs = (g.astype(f32) * scale_rows[l, span(h)]).astype(bf16)
        gs_all[l, span(h)] = gs
        delta = jnp.sum(gs.astype(f32) * og[l, 0, :, cols(h)].astype(f32), axis=-1, keepdims=True)
        return nt(gs, values(l)), delta

    def scores_grad(l, h, dp, delta):
        ds = (expo[l, span(h)].astype(f32) * (dp - delta)).astype(bf16)
        ds_all[l, span(h)] = ds
        return ds

    def query_grad(l, h, ds):
        og[l, 1, :, cols(h)] = (nn(ds, keys(l)) * SCALE).astype(bf16)
        if h == heads - 1:
            gk = nn(queries[l].T, ds_all[l]) * SCALE
            gv = nn(gs_all[l].T, expo[l])
            dkv[0, l] = gk.T.astype(bf16).reshape(NEAR * TILES, CORES, TILE, HEAD_DIM)
            dkv[1, l] = gv.T.astype(bf16).reshape(NEAR * TILES, CORES, TILE, HEAD_DIM)

    steps = [(l, h) for l in reversed(range(layers)) for h in range(heads)]
    first, second = {}, {}
    for i in range(len(steps) + 2):
        if i < len(steps):
            first[i] = probs_grad(*steps[i])
        if 1 <= i <= len(steps):
            second[i - 1] = scores_grad(*steps[i - 1], *first.pop(i - 1))
        if i >= 2:
            query_grad(*steps[i - 2], second.pop(i - 2))

    pairs = []
    for d in range(layers):
        l = lax.rem(pipe + d, layers)
        for k in range(2):
            pairs.append((dkv.at[k, l, :, 1 - core], give.at[d, k]))
            pairs.append((dkv.at[k, l, :, core], keep.at[d, k]))
    for m, x in enumerate((og0, og1, og2, og3)):
        pairs.append((og.at[layer_of(m)], x))
    run_copies(pairs, out_sems)


def run_layers(bias, mine, theirs, qc_parts):
    _, rows, width = qc_parts[0].shape
    stacked = rows * width // HEAD_DIM
    kv_shape = shape(LAYERS, 2, NEAR * TILES, TILE, HEAD_DIM)
    return pl.pallas_call(
        layers_kernel,
        out_shape=(kv_shape, kv_shape) + (shape(2, rows, width),) * LAYERS,
        in_specs=[ANY] * 13,
        out_specs=(ANY,) * 6,
        scratch_shapes=[
            pltpu.VMEM((rows, SPAN), f32),
            pltpu.VMEM((2, LAYERS, NEAR * TILES, CORES, TILE, HEAD_DIM), bf16),
            pltpu.VMEM((LAYERS, 2, rows, width), bf16),
            pltpu.VMEM((LAYERS, 2, rows, width), bf16),
            pltpu.VMEM((2, LAYERS, NEAR * TILES, CORES, TILE, HEAD_DIM), bf16),
            pltpu.VMEM((LAYERS, stacked, SPAN), bf16),
            pltpu.VMEM((LAYERS, stacked, HEAD_DIM), bf16),
            pltpu.VMEM((LAYERS, stacked, HEAD_DIM), f32),
            pltpu.VMEM((LAYERS, stacked, HEAD_DIM), bf16),
            pltpu.VMEM((LAYERS, stacked, SPAN), bf16),
            pltpu.SemaphoreType.DMA((21,)),
            pltpu.SemaphoreType.DMA((20,)),
        ],
        compiler_params=PARAMS,
        name="layers",
    )(bias, *mine, *theirs, *qc_parts)


def place_kernel(
    order_in, p0, p1, p2, p3, sent_out, order, parts, sent, order_sem, sems, out_sems
):
    pipe, _, _ = place_of()
    order_copy = pltpu.make_async_copy(order_in, order, order_sem)
    order_copy.start()
    copies = [
        pltpu.make_async_copy(
            x, parts.at[lax.rem(pipe + LAYERS - d, LAYERS)], sems.at[d]
        )
        for d, x in enumerate((p0, p1, p2, p3))
    ]
    for copy in copies:
        copy.start()
    sent[...] = jnp.zeros(sent.shape, bf16)
    order_copy.wait()
    first = order[lax.axis_index("ctx")] - REACH
    outs = [
        pltpu.make_async_copy(sent.at[:, c], sent_out.at[:, c], out_sems.at[c])
        for c in range(sent.shape[1])
    ]
    steps = [order[c] - first for c in range(sent.shape[1])]
    nears = [(j >= 0) & (j <= REACH) for j in steps]
    for near, out in zip(nears, outs):

        @pl.when(jnp.logical_not(near))
        def _(out=out):
            out.start()

    for copy in copies:
        copy.wait()
    for c, (j, near, out) in enumerate(zip(steps, nears, outs)):

        @pl.when(near)
        def _(c=c, j=j, out=out):
            at = pl.ds(j * TILES, TILES)
            for head in range(2):
                total = parts[2 * head, :, at].astype(f32) + parts[2 * head + 1, :, at].astype(f32)
                total = total.astype(bf16)
                for k in range(2):
                    sent[:, c, k, head] = total[k]
            out.start()

    for out in outs:
        out.wait()


def place(order, parts):
    return pl.pallas_call(
        place_kernel,
        out_shape=shape(TILES, order.shape[0], 2, 2, TILE, HEAD_DIM),
        in_specs=[ANY] * (1 + LAYERS),
        out_specs=ANY,
        scratch_shapes=[
            pltpu.SMEM(order.shape, jnp.int32),
            pltpu.VMEM((LAYERS,) + parts[0].shape, bf16),
            pltpu.VMEM((TILES, order.shape[0], 2, 2, TILE, HEAD_DIM), bf16),
            pltpu.SemaphoreType.DMA,
            pltpu.SemaphoreType.DMA((LAYERS,)),
            pltpu.SemaphoreType.DMA(order.shape),
        ],
        compiler_params=PARAMS,
        name="place",
    )(order, *parts)


def total_kernel(got_in, grad_key, grad_value, got, sems):
    copies = [
        pltpu.make_async_copy(got_in.at[x], got.at[x], sems.at[x]) for x in range(TILES)
    ]
    for copy in copies:
        copy.start()
    for x in range(TILES):
        copies[x].wait()
        total = got[x, 0].astype(f32)
        for c in range(1, got.shape[1]):
            total = total + got[x, c].astype(f32)
        total = total.astype(bf16)
        for kind, whole in enumerate((grad_key, grad_value)):
            for j in range(2):
                head = 2 * x + j
                whole[:, head * HEAD_DIM:(head + 1) * HEAD_DIM] = total[kind, j]


def total(got):
    return pl.pallas_call(
        total_kernel,
        out_shape=(shape(TILE, TILES * 2 * HEAD_DIM),) * 2,
        in_specs=[ANY],
        out_specs=(VMEM, VMEM),
        scratch_shapes=[pltpu.VMEM(got.shape, bf16), pltpu.SemaphoreType.DMA((TILES,))],
        compiler_params=PARAMS,
        name="total",
    )(got)


def assemble_kernel(g0, g1, g2, g3, out, grad_query, sems):
    width = g0.shape[2]
    pairs = []
    for m, piece in enumerate((g0, g1, g2, g3)):
        column = pl.multiple_of(group_of(m) * width, width)
        for i, whole in enumerate((out, grad_query)):
            pairs.append((piece.at[i], whole.at[:, pl.ds(column, width)]))
    run_copies(pairs, sems)


def assemble(pieces):
    _, rows, width = pieces[0].shape
    return pl.pallas_call(
        assemble_kernel,
        out_shape=(shape(rows, LAYERS * width),) * 2,
        in_specs=[ANY] * 4,
        out_specs=(ANY, ANY),
        scratch_shapes=[pltpu.SemaphoreType.DMA((8,))],
        compiler_params=PARAMS,
        name="assemble",
    )(*pieces)


def moved(block, distance):
    size = lax.axis_size("pipe")
    return lax.ppermute(block, "pipe", [(i, (i + distance) % size) for i in range(size)])


def swapped(block):
    size = lax.axis_size("tp")
    return lax.ppermute(block, "tp", [(i, i ^ 1) for i in range(size)])


def sent_over(block, pairs):
    tp_count = lax.axis_size("tp")
    route = [
        (a * tp_count + x + b, c * tp_count + x + d)
        for (a, b), (c, d) in pairs
        for x in range(0, tp_count, CORES)
    ]
    return lax.ppermute(block, ("pipe", "tp"), route)


def round_pairs(m):
    pairs = []
    for l in range(LAYERS):
        for core in range(CORES):
            group = GROUP_OF[m][(l + 2 * core) % LAYERS]
            pairs.append(((l, core), (2 * core + group // CORES, group % CORES)))
    return pairs


def exchanged(block):
    ctx_count, tp_count = lax.axis_size("ctx"), lax.axis_size("tp")
    groups = [
        [c * tp_count + tp for c in range(ctx_count) for tp in range(core, tp_count, CORES)]
        for core in range(CORES)
    ]
    flat = block.reshape(TILES * ctx_count, -1, HEAD_DIM)
    got = lax.all_to_all(
        flat, ("ctx", "tp"), split_axis=0, concat_axis=0, axis_index_groups=groups, tiled=True
    )
    return got.reshape(block.shape)


def exchanged_by_x(block):
    ctx_count, tp_count = lax.axis_size("ctx"), lax.axis_size("tp")
    groups = [
        [c * tp_count + tp for tp in range(core, tp_count, CORES) for c in range(ctx_count)]
        for core in range(CORES)
    ]
    flat = block.reshape(TILES * ctx_count, -1, HEAD_DIM)
    got = lax.all_to_all(
        flat, ("ctx", "tp"), split_axis=0, concat_axis=0, axis_index_groups=groups, tiled=True
    )
    return got.reshape(block.shape)


def cut(block, starts, sizes):
    return lax.dynamic_slice(block, starts, sizes, allow_negative_indices=False)


def shards(query_in, key_in, value_in, doc_ids, stretch_order, out_cot):
    ctx_count = lax.axis_size("ctx")
    layer = lax.axis_index("pipe")
    rows = query_in.shape[1]

    got = exchanged(spread(jnp.concatenate([key_in, value_in]), ctx_count))
    pieces = pieces_of(query_in[0], out_cot[0])
    qc_parts = [sent_over(pieces[m], round_pairs(m)) for m in range(LAYERS)]

    position = stretch_order[lax.axis_index("ctx")]
    block_ids = jnp.arange(ctx_count, dtype=jnp.int32)
    wanted = jnp.maximum(position - REACH + jnp.arange(NEAR, dtype=jnp.int32), 0)
    holder = jnp.sum(
        jnp.where(stretch_order[None, :] == wanted[:, None], block_ids[None, :], 0), axis=1
    )

    def window(distance):
        head = lax.rem(layer + distance, LAYERS) // 2
        return jnp.concatenate(
            [
                cut(got, (holder[j] * TILES, 0, head, 0, 0), (TILES, 2, 1, TILE, HEAD_DIM))
                for j in range(NEAR)
            ]
        ).reshape(NEAR * TILES, 2, TILE, HEAD_DIM)

    mine = [window(0)] + [moved(window(d), d) for d in (1, 3, 2)]
    mine = [mine[0], mine[1], mine[3], mine[2]]
    theirs = [swapped(x) for x in mine]

    offsets = jnp.arange(SPAN, dtype=jnp.int32)
    row_ids = jnp.arange(rows, dtype=jnp.int32)
    documents = jnp.concatenate([jnp.full((REACH * BLOCK,), -1, jnp.int32), doc_ids])
    near_documents = cut(documents, (position * BLOCK,), (SPAN,))
    own_documents = near_documents[REACH * BLOCK:]
    allowed = (offsets[None, :] <= row_ids[:, None] + REACH * BLOCK) & (
        near_documents[None, :] == own_documents[:, None]
    )
    bias = jnp.where(allowed, 0.0, masked_score).astype(f32)

    keep, give, *groups = run_layers(bias, mine, theirs, qc_parts)
    received = swapped(give)
    sums = [
        (keep[d].astype(f32) + received[d].astype(f32)).astype(bf16) for d in range(LAYERS)
    ]
    parts = [sums[0]] + [moved(sums[d], d) for d in (1, 3, 2)]
    parts = [parts[0], parts[1], parts[3], parts[2]]
    grad_key, grad_value = total(exchanged_by_x(place(stretch_order, parts)))
    out, grad_query = assemble(
        [
            sent_over(groups[m], [(b, a) for a, b in round_pairs(m)]) for m in range(LAYERS)
        ]
    )
    return (out[None], grad_query[None], grad_key[None], grad_value[None])


def solution(mesh):
    return jax.shard_map(
        shards,
        mesh=mesh,
        in_specs=(
            P("pipe", "ctx", "tp"),
            P("pipe", ("ctx", "tp"), None),
            P("pipe", ("ctx", "tp"), None),
            P(),
            P(),
            P("pipe", "ctx", "tp"),
        ),
        out_specs=(
            P("pipe", "ctx", "tp"),
            P("pipe", "ctx", "tp"),
            P("pipe", ("ctx", "tp"), None),
            P("pipe", ("ctx", "tp"), None),
        ),
        check_vma=False,
    )
```
